32 devices in a mesh: dp: 8 (over y, x, core), tensor: 4 (over z).
Axes of the slice: x: 2, y: 2, z: 4, core: 2. Of those that a mesh axis runs over, the one named last changes fastest.
Arguments:
- hidden: bfloat16 [4096, 8192], P(('dp', 'tensor')), may hold values from -6 to 6
- norm_gain: float32 [8192], replicated, may hold values from 0.5 to 1.5
- tile_values: bfloat16 [4, 80, 128, 128], P('tensor', 'dp'), may hold values from -0.15625 to 0.15625
- tile_ids: int32 [4, 80], P('tensor', 'dp'), may hold values from 0 to 1279, as said below
- tile_counts: int32 [4, 8], P('tensor', 'dp'), may hold values from 5 to 10, as said below
- proj_grad: bfloat16 [4096, 10240], P('dp', 'tensor'), may hold values from -6 to 6
Outputs:
- projections: bfloat16 [4096, 10240], P('dp', 'tensor')
- hidden_grad: bfloat16 [4096, 8192], P(('dp', 'tensor'))
- tile_grads: float32 [4, 80, 128, 128], P('tensor', 'dp')
- gain_grad: float32 [8192], replicated
The draws below stay inside these ranges and needn't reach their ends.
Inputs may be any that keep to these rules, and one draw needn't show every extreme that they name: `tile_ids`: within each tensor index the 80 block numbers are distinct; a slot's number holds whether or not the slot is live. `tile_counts`: for every tensor index some owner has all 10 slots live.
All inputs are finite; a program needn't handle non-finite values.
Results may differ from the reference program's by a relative error of at most 0.013.
Values may be sent and summed in bfloat16 or wider, within the bound.
A program may use at most 192 MiB of HBM per device.

```python
import jax
import jax.numpy as jnp
from jax import lax

D = 8192
TILE = 128
SLOTS = 10
QKV = 10240
SEQ = 512
TOKENS = 4096
N_DP = 8
N_TENSOR = 4


def draw_tile_ids(key, part):
    per_rank = D // TILE * (QKV // N_TENSOR // TILE)
    rank_keys = jax.random.split(key, N_TENSOR)

    def one_rank(rank_key):
        return jax.random.permutation(rank_key, per_rank)[:N_DP * SLOTS]
    return jax.vmap(one_rank)(rank_keys).astype(jnp.int32)


def draw_tile_counts(key, part):
    base = jax.random.randint(key, (N_TENSOR, N_DP), SLOTS // 2, SLOTS + 1)
    fullest = jax.random.randint(jax.random.fold_in(key, 7), (N_TENSOR, 1), 0, N_DP)
    owners = jnp.arange(N_DP, dtype=jnp.int32)[None, :]
    return jnp.where(owners == fullest, SLOTS, base).astype(jnp.int32)


def level_of(key, dims, pieces, low, largest):
    def one(axis_at, shards_of):
        draws = jax.random.uniform(jax.random.fold_in(jax.random.fold_in(key, 6), axis_at), (shards_of,), jnp.float32, low / len(pieces), largest / len(pieces))
        return jnp.repeat(jnp.exp(draws), dims[axis_at] // shards_of).reshape((-1,) + (1,) * (len(dims) - axis_at - 1))

    loudness = one(*pieces[0])
    for cut in pieces[1:]:
        loudness = loudness * one(*cut)
    return loudness


def gaussian(stream_key, extent, spread, most, pieces=(), held_as=jnp.bfloat16):
    loudness = level_of(stream_key, extent, pieces, -0.22, 0.18) if pieces else 1.0
    drawn = jax.random.normal(stream_key, extent, jnp.float32) * spread * loudness
    return jnp.minimum(jnp.maximum(drawn, -most), most).astype(held_as)


def setup_inputs(seed: int = 0) -> dict:
    key_of = jax.random.split(jax.random.key(seed), 7)
    return {
        "hidden": gaussian(key_of[0], (TOKENS, D), 1.0, 6.0, ((0, 32),)),
        "norm_gain": jnp.clip(1.0 + 0.1 * jax.random.normal(key_of[1], (D,), jnp.float32), 0.5, 1.5),
        "tile_values": gaussian(key_of[2], (N_TENSOR, N_DP * SLOTS, TILE, TILE), (D // 5) ** -0.5, 0.15625, ((0, 4), (1, 8))),
        "tile_ids": draw_tile_ids(jax.random.fold_in(key_of[6], 71), 0),
        "tile_counts": draw_tile_counts(jax.random.fold_in(key_of[6], 71), 0),
        "proj_grad": gaussian(key_of[5], (TOKENS, QKV), 1.0, 6.0, ((0, 8), (1, 4))),
    }


EPSILON = 1e-05

def reference(hidden, norm_gain, tile_values, tile_ids, tile_counts, proj_grad):
    hidden_f = hidden.astype(jnp.float32)
    inverse = lax.rsqrt(lax.optimization_barrier(jnp.mean(hidden_f * hidden_f, axis=-1, keepdims=True)) + EPSILON)
    normed = (hidden_f * inverse * norm_gain).astype(jnp.bfloat16)
    row_tiles = D // TILE
    col_tiles = QKV // N_TENSOR // TILE
    total_slots = N_DP * SLOTS
    slot_index = jnp.arange(total_slots, dtype=jnp.int32)
    normed_groups = normed.reshape(N_DP, SEQ, D)
    grad_ranks = proj_grad.reshape(N_DP, SEQ, N_TENSOR, col_tiles * TILE).transpose(2, 0, 1, 3)

    def per_rank(grad_total, rank_input):
        block_vals, block_names, counts, grad_groups = rank_input
        live_mask = (slot_index % SLOTS < counts[slot_index // SLOTS]).astype(jnp.float32)
        weights = block_vals.astype(jnp.float32) * live_mask[:, None, None]
        tile_rows = block_names // col_tiles
        tile_cols = block_names % col_tiles

        def per_group(weight_total, group_input):
            group_rows, group_grads = group_input
            picked_x = group_rows.reshape(SEQ, row_tiles, TILE)[:, tile_rows, :].astype(jnp.float32)
            picked_g = group_grads.reshape(SEQ, col_tiles, TILE)[:, tile_cols, :].astype(jnp.float32)
            forward = jnp.einsum('nsi,sij->nsj', picked_x, weights)
            outputs = jnp.zeros((SEQ, col_tiles, TILE), jnp.float32).at[:, tile_cols, :].add(forward)
            backward = jnp.einsum('nsj,sij->nsi', picked_g, weights)
            row_part = jnp.zeros((SEQ, row_tiles, TILE), jnp.float32).at[:, tile_rows, :].add(backward)
            tile_part = jnp.einsum('nsi,nsj->sij', picked_x, picked_g)
            tile_part = lax.optimization_barrier(tile_part.astype(jnp.bfloat16)).astype(jnp.float32)
            return (weight_total + tile_part, (outputs.reshape(SEQ, col_tiles * TILE).astype(jnp.bfloat16), row_part.reshape(SEQ, D).astype(jnp.bfloat16)))
        weight_start = jnp.zeros((total_slots, TILE, TILE), jnp.float32)
        weight_total, (outputs, row_parts) = lax.scan(per_group, weight_start, (normed_groups, grad_groups))
        grad_total = grad_total + row_parts.reshape(TOKENS, D).astype(jnp.float32)
        return (grad_total, (outputs.reshape(TOKENS, col_tiles * TILE), weight_total * live_mask[:, None, None]))
    grad_start = jnp.zeros((TOKENS, D), jnp.float32)
    row_grad, (rank_outputs, tile_grads) = lax.scan(per_rank, grad_start, (tile_values, tile_ids, tile_counts, grad_ranks))
    projections = rank_outputs.transpose(1, 0, 2).reshape(TOKENS, QKV)
    unit = hidden_f * inverse
    gain_grad = lax.optimization_barrier(jnp.sum(row_grad * unit, axis=0))
    scaled = row_grad * norm_gain
    hidden_grad = (inverse * (scaled - unit * lax.optimization_barrier(jnp.mean(scaled * unit, axis=-1, keepdims=True)))).astype(jnp.bfloat16)
    return (projections, hidden_grad, tile_grads, gain_grad)
```

```python
import functools

import jax
import jax.numpy as jnp
from jax import lax
from jax.experimental import pallas as pl
from jax.experimental.pallas import tpu as pltpu
from jax.sharding import PartitionSpec as P

EPSILON = 1e-05
VMEM_BYTES = 56 * 1024 * 1024


def lanes(block, tile):
    return pl.ds(pl.multiple_of(block * tile, tile), tile)


def project_kernel(ids_ref, x_ref, w_ref, out_ref, acc_ref, *, cols):
    owners, _, slots, tile, _ = w_ref.shape
    t = pl.program_id(0)
    acc_ref[...] = jnp.zeros_like(acc_ref)

    def owner_step(owner, carry):
        parts = []
        for s in range(slots):
            block = ids_ref[owner, t, s]
            left = x_ref[:, lanes(block // cols, tile)]
            parts.append(jnp.dot(left, w_ref[owner, 0, s], preferred_element_type=jnp.float32))
        for s in range(slots):
            place = lanes(ids_ref[owner, t, s] % cols, tile)
            acc_ref[:, place] += parts[s]
        return carry

    lax.fori_loop(0, owners, owner_step, 0)
    out_ref[0] = acc_ref[...].astype(out_ref.dtype)


def gradient_kernel(
    ids_ref, xt_ref, w_ref, g_ref, h_ref, inv_ref, gain_ref,
    tiles_ref, hgrad_ref, gpart_ref, acc_ref, *, cols,
):
    owners, _, slots, tile, _ = w_ref.shape
    tokens, width = acc_ref.shape
    t = pl.program_id(0)

    @pl.when(t == 0)
    def _():
        acc_ref[...] = jnp.zeros_like(acc_ref)

    def owner_step(owner, carry):
        parts = []
        for s in range(slots):
            block = ids_ref[owner, t, s]
            g = g_ref[0, :, lanes(block % cols, tile)]
            parts.append(
                lax.dot_general(
                    g, w_ref[owner, 0, s], (((1,), (1,)), ((), ())),
                    preferred_element_type=jnp.float32,
                )
            )
            left = xt_ref[lanes(block // cols, tile), :]
            tiles_ref[owner, 0, s] = jnp.dot(left, g, preferred_element_type=jnp.float32).astype(
                tiles_ref.dtype
            )
        for s in range(slots):
            place = lanes(ids_ref[owner, t, s] // cols, tile)
            acc_ref[:, place] += parts[s]
        return carry

    lax.fori_loop(0, owners, owner_step, 0)

    @pl.when(t == pl.num_programs(0) - 1)
    def _():
        rows = 16
        gpart_ref[...] = jnp.zeros_like(gpart_ref)

        def row_step(i, carry):
            at = pl.ds(pl.multiple_of(i * rows, rows), rows)
            inverse = inv_ref[at, :]
            unit = h_ref[at, :].astype(jnp.float32) * inverse
            row_grad = acc_ref[at, :]
            product = row_grad * unit
            gpart_ref[...] += jnp.sum(product, axis=0, keepdims=True)
            mean = jnp.mean(product * gain_ref[...], axis=-1, keepdims=True)
            hgrad_ref[at, :] = (
                inverse * (row_grad * gain_ref[...] - unit * mean)
            ).astype(hgrad_ref.dtype)
            return carry

        lax.fori_loop(0, tokens // rows, row_step, 0)


def body(hidden, norm_gain, tile_values, tile_ids, tile_counts, proj_grad):
    tokens, width = hidden.shape
    _, slots, tile, _ = tile_values.shape
    seq, part_cols = proj_grad.shape
    cols = part_cols // tile
    n_tensor = lax.axis_size("tensor")
    n_dp = lax.axis_size("dp")
    live = jnp.arange(slots) < tile_counts[0, 0]
    masked = jnp.where(live[:, None, None], tile_values[0], 0)

    ids = lax.all_gather(tile_ids[0], ("dp", "tensor"), axis=0, tiled=False)
    ids = ids.reshape(n_dp, n_tensor, slots)
    line = lax.all_gather(masked, "tensor", axis=0, tiled=False)
    weights = lax.all_gather(line, "dp", axis=0, tiled=False)
    grads = lax.all_to_all(
        proj_grad.reshape(n_tensor, tokens, part_cols), "tensor", split_axis=0, concat_axis=0
    )

    hidden_f = hidden.astype(jnp.float32)
    inverse = lax.rsqrt(jnp.mean(hidden_f * hidden_f, axis=-1, keepdims=True) + EPSILON)
    normed = (hidden_f * inverse * norm_gain).astype(jnp.bfloat16)
    flipped = normed.T

    whole = lambda *shape: pl.BlockSpec(shape, lambda t, ids: (0,) * len(shape))
    w_spec = pl.BlockSpec((n_dp, 1, slots, tile, tile), lambda t, ids: (0, t, 0, 0, 0))
    c_spec = pl.BlockSpec((1, tokens, part_cols), lambda t, ids: (t, 0, 0))
    total = n_dp * n_tensor * slots
    flops = 2 * total * tokens * tile * tile
    params = pltpu.CompilerParams(
        dimension_semantics=("arbitrary",), vmem_limit_bytes=VMEM_BYTES
    )
    projected = pl.pallas_call(
        functools.partial(project_kernel, cols=cols),
        out_shape=jax.ShapeDtypeStruct((n_tensor, tokens, part_cols), jnp.bfloat16),
        grid_spec=pltpu.PrefetchScalarGridSpec(
            num_scalar_prefetch=1,
            grid=(n_tensor,),
            in_specs=[whole(tokens, width), w_spec],
            out_specs=c_spec,
            scratch_shapes=[pltpu.VMEM((tokens, part_cols), jnp.float32)],
        ),
        compiler_params=params,
        cost_estimate=pl.CostEstimate(
            flops=4 * flops, bytes_accessed=2 * total * tile * tile, transcendentals=0
        ),
        name="project",
    )(ids, normed, weights)
    projections = lax.all_to_all(projected, "tensor", split_axis=0, concat_axis=0)
    projections = projections.reshape(seq, part_cols)

    tile_parts, hidden_grad, gain_part = pl.pallas_call(
        functools.partial(gradient_kernel, cols=cols),
        out_shape=(
            jax.ShapeDtypeStruct((n_dp, n_tensor, slots, tile, tile), jnp.bfloat16),
            jax.ShapeDtypeStruct((tokens, width), jnp.bfloat16),
            jax.ShapeDtypeStruct((1, width), jnp.float32),
        ),
        grid_spec=pltpu.PrefetchScalarGridSpec(
            num_scalar_prefetch=1,
            grid=(n_tensor,),
            in_specs=[
                whole(width, tokens), w_spec, c_spec, whole(tokens, width),
                whole(tokens, 1), whole(1, width),
            ],
            out_specs=[w_spec, whole(tokens, width), whole(1, width)],
            scratch_shapes=[pltpu.VMEM((tokens, width), jnp.float32)],
        ),
        compiler_params=params,
        cost_estimate=pl.CostEstimate(
            flops=8 * flops, bytes_accessed=4 * total * tile * tile, transcendentals=0
        ),
        name="gradient",
    )(ids, flipped, weights, grads, hidden, inverse, norm_gain[None, :])

    plane = lax.psum_scatter(tile_parts, "dp", scatter_dimension=0, tiled=False)
    tile_sum = lax.psum_scatter(plane, "tensor", scatter_dimension=0, tiled=False)
    tile_grads = jnp.where(live[:, None, None], tile_sum.astype(jnp.float32), 0.0)[None]
    gain_grad = lax.psum(gain_part[0], ("dp", "tensor"))
    return (projections, hidden_grad, tile_grads, gain_grad)


def solution(mesh):
    in_specs = (
        P(("dp", "tensor"), None),
        P(),
        P("tensor", "dp", None, None),
        P("tensor", "dp"),
        P("tensor", "dp"),
        P("dp", "tensor"),
    )
    out_specs = (P("dp", "tensor"), P(("dp", "tensor"), None), P("tensor", "dp", None, None), P())
    return jax.shard_map(body, mesh=mesh, in_specs=in_specs, out_specs=out_specs, check_vma=False)
```

```python
import functools

import jax
import jax.numpy as jnp
from jax import lax
from jax.experimental import pallas as pl
from jax.experimental.pallas import tpu as pltpu
from jax.sharding import PartitionSpec as P

EPSILON = 1e-05
VMEM_BYTES = 56 * 1024 * 1024
MESH = pl.DeviceIdType.MESH
TAIL = 16


def lanes(block, tile):
    return pl.ds(pl.multiple_of(block * tile, tile), tile)


def spread_kernel(
    tiles_ref, g_ref, h_ref, gain_ref,
    w_ref, grads_ref, x_ref, xt_ref, inv_ref,
    z_send, z_recv, p_send, p_recv, c_send, c_recv, a_send, a_recv, l_sem,
    *, pairs, n_tensor, tile,
):
    d = lax.axis_index("dp")
    t = lax.axis_index("tensor")
    core = lax.rem(d, 2)
    pair = d // 2
    other = pair * 2 + 1 - core

    def line(k):
        return lax.rem(t + k + n_tensor, n_tensor)

    def peer(j):
        return lax.rem(pair + j + pairs, pairs) * 2 + core

    greet(d, t, other, peer, line, pairs, n_tensor)

    def remote(src, dst, send, recv, to):
        return pltpu.make_async_remote_copy(
            src_ref=src, dst_ref=dst, send_sem=send, recv_sem=recv,
            device_id=to, device_id_type=MESH,
        )

    def over_line(k):
        return remote(
            tiles_ref, w_ref.at[d, t], z_send.at[k], z_recv.at[k], (d, line(k))
        )

    def over_plane(k, j):
        slot = w_ref.at[d, line(-k)]
        src = tiles_ref if k == 0 else slot
        return remote(src, slot, p_send.at[k, j], p_recv.at[k, j], (peer(j), t))

    def over_core(k, j):
        slot = w_ref.at[peer(-j), line(-k)]
        src = tiles_ref if k == 0 and j == 0 else slot
        return remote(src, slot, c_send.at[k, j], c_recv.at[k, j], (other, t))

    def exchange(k):
        return remote(
            g_ref.at[line(k)], grads_ref.at[t], a_send.at[k], a_recv.at[k], (d, line(k))
        )

    def landed(slot, send, recv):
        remote(slot, slot, send, recv, (other, t)).wait_recv()

    for k in range(1, n_tensor):
        over_line(k).start()
    for j in range(1, pairs):
        over_plane(0, j).start()
    over_core(0, 0).start()
    own = (
        pltpu.make_async_copy(tiles_ref, w_ref.at[d, t], l_sem.at[0]),
        pltpu.make_async_copy(g_ref.at[t], grads_ref.at[t], l_sem.at[1]),
    )
    for copy in own:
        copy.start()

    tokens, width = h_ref.shape
    rows = 16

    def norm_step(i, carry):
        at = pl.ds(pl.multiple_of(i * rows, rows), rows)
        hidden = h_ref[at, :].astype(jnp.float32)
        inverse = lax.rsqrt(jnp.mean(hidden * hidden, axis=-1, keepdims=True) + EPSILON)
        inv_ref[at, :] = inverse
        x_ref[at, :] = (hidden * inverse * gain_ref[...]).astype(x_ref.dtype)
        return carry

    lax.fori_loop(0, tokens // rows, norm_step, 0)

    for k in range(1, n_tensor):
        landed(w_ref.at[d, line(-k)], z_send.at[k], z_recv.at[k])
        for j in range(1, pairs):
            over_plane(k, j).start()
        over_core(k, 0).start()
    for k in range(1, n_tensor):
        exchange(k).start()

    def flip_step(i, carry):
        at = lanes(i, tile)
        xt_ref[at, :] = x_ref[:, at].astype(jnp.float32).T.astype(xt_ref.dtype)
        return carry

    lax.fori_loop(0, width // tile, flip_step, 0)

    for k in range(n_tensor):
        for j in range(1, pairs):
            landed(w_ref.at[peer(-j), line(-k)], p_send.at[k, j], p_recv.at[k, j])
            over_core(k, j).start()
    for k in range(n_tensor):
        for j in range(pairs):
            far = lax.rem(pair - j + pairs, pairs) * 2 + 1 - core
            landed(w_ref.at[far, line(-k)], c_send.at[k, j], c_recv.at[k, j])
    for k in range(1, n_tensor):
        landed(grads_ref.at[line(-k)], a_send.at[k], a_recv.at[k])
    for copy in own:
        copy.wait()
    for k in range(n_tensor):
        if k:
            over_line(k).wait_send()
            exchange(k).wait_send()
        for j in range(pairs):
            if j:
                over_plane(k, j).wait_send()
            over_core(k, j).wait_send()


def greet(d, t, other, peer, line, pairs, n_tensor):
    barrier = pltpu.get_barrier_semaphore()
    targets = [(other, t)]
    targets += [(peer(j), t) for j in range(1, pairs)]
    targets += [(d, line(k)) for k in range(1, n_tensor)]
    for target in targets:
        pl.semaphore_signal(barrier, inc=1, device_id=target, device_id_type=MESH)
    pl.semaphore_wait(barrier, len(targets))


def collect_kernel(
    parts_ref, out_in_ref, gain_ref, sum_ref, out_ref, total_ref,
    mine, from_core, from_plane, from_line, g_core, g_plane, g_line,
    c_send, c_recv, p_send, p_recv, z_send, z_recv, a_send, a_recv,
    gc_send, gc_recv, gp_send, gp_recv, gz_send, gz_recv, l_sem, o_sem,
    *, pairs, n_tensor, tile,
):
    d = lax.axis_index("dp")
    t = lax.axis_index("tensor")
    core = lax.rem(d, 2)
    pair = d // 2
    other = pair * 2 + 1 - core

    def line(k):
        return lax.rem(t + k + n_tensor, n_tensor)

    def near(j):
        return lax.rem(pair + j + pairs, pairs)

    def peer(j):
        return near(j) * 2 + core

    greet(d, t, other, peer, line, pairs, n_tensor)

    def remote(src, dst, send, recv, to):
        return pltpu.make_async_remote_copy(
            src_ref=src, dst_ref=dst, send_sem=send, recv_sem=recv,
            device_id=to, device_id_type=MESH,
        )

    def over_core(j):
        return remote(
            parts_ref.at[near(j) * 2 + 1 - core], from_core.at[near(j)],
            c_send.at[j], c_recv.at[j], (other, t),
        )

    def load_own(j):
        return pltpu.make_async_copy(parts_ref.at[peer(j)], mine.at[near(j)], l_sem.at[j])

    def over_plane(j, k):
        return remote(
            mine.at[near(j), line(k)], from_plane.at[pair, line(k)],
            p_send.at[j, k], p_recv.at[j, k], (peer(j), t),
        )

    def over_line(k):
        return remote(
            mine.at[pair, line(k)], from_line.at[k], z_send.at[k], z_recv.at[k], (d, line(k))
        )

    def exchange(k):
        return remote(
            out_in_ref.at[line(k)], out_ref.at[t], a_send.at[k], a_recv.at[k], (d, line(k))
        )

    def landed(slot, send, recv):
        remote(slot, slot, send, recv, (other, t)).wait_recv()

    order = list(range(1, pairs)) + [0]
    gain_core = remote(gain_ref, g_core, gc_send, gc_recv, (other, t))
    gain_core.start()
    for j in order:
        over_core(j).start()
        load_own(j).start()
    for k in range(1, n_tensor):
        exchange(k).start()
    own_out = pltpu.make_async_copy(out_in_ref.at[t], out_ref.at[t], o_sem)
    own_out.start()

    gain_core.wait_recv()
    g_plane[pair] = gain_ref[...] + g_core[...]
    gain_plane = [
        remote(g_plane.at[pair], g_plane.at[pair], gp_send.at[j], gp_recv.at[j], (peer(j), t))
        for j in range(1, pairs)
    ]
    for copy in gain_plane:
        copy.start()

    steps = mine.shape[2] // tile
    f32 = jnp.float32
    lines = list(range(1, n_tensor)) + [0]
    for j in range(1, pairs):
        load_own(j).wait()
        landed(from_core.at[near(j)], c_send.at[j], c_recv.at[j])
        for k in lines:

            def core_step(i, carry, j=j, k=k):
                at = lanes(i, tile)
                both = mine[near(j), line(k), at, :].astype(f32)
                both += from_core[near(j), line(k), at, :].astype(f32)
                mine[near(j), line(k), at, :] = both.astype(mine.dtype)
                return carry

            lax.fori_loop(0, steps, core_step, 0)
            over_plane(j, k).start()
    load_own(0).wait()
    landed(from_core.at[pair], c_send.at[0], c_recv.at[0])

    for j in range(1, pairs):
        landed(g_plane.at[near(-j)], gp_send.at[j], gp_recv.at[j])
    whole_plane = g_plane[0]
    for p in range(1, pairs):
        whole_plane += g_plane[p]
    g_line[t] = whole_plane
    gain_line = [
        remote(g_line.at[t], g_line.at[t], gz_send.at[k], gz_recv.at[k], (d, line(k)))
        for k in range(1, n_tensor)
    ]
    for copy in gain_line:
        copy.start()

    for k in lines:
        for j in range(1, pairs):
            landed(from_plane.at[near(-j), line(k)], p_send.at[j, k], p_recv.at[j, k])

        def plane_step(i, carry, k=k):
            at = lanes(i, tile)
            total = mine[pair, line(k), at, :].astype(f32)
            total += from_core[pair, line(k), at, :].astype(f32)
            for j in range(1, pairs):
                total += from_plane[near(-j), line(k), at, :].astype(f32)
            if k:
                mine[pair, line(k), at, :] = total.astype(mine.dtype)
            else:
                sum_ref[at, :] = total
            return carry

        lax.fori_loop(0, steps, plane_step, 0)
        if k:
            over_line(k).start()

    for k in range(1, n_tensor):
        landed(g_line.at[line(-k)], gz_send.at[k], gz_recv.at[k])
    whole_line = g_line[0]
    for q in range(1, n_tensor):
        whole_line += g_line[q]
    total_ref[...] = whole_line

    for k in range(1, n_tensor):
        landed(from_line.at[k], z_send.at[k], z_recv.at[k])

    def line_step(i, carry):
        at = lanes(i, tile)
        total = sum_ref[at, :]
        for k in range(1, n_tensor):
            total += from_line[k, at, :].astype(f32)
        sum_ref[at, :] = total
        return carry

    lax.fori_loop(0, steps, line_step, 0)

    for k in range(1, n_tensor):
        landed(out_ref.at[line(-k)], a_send.at[k], a_recv.at[k])
    own_out.wait()
    gain_core.wait_send()
    for copy in gain_plane + gain_line:
        copy.wait_send()
    for j in range(pairs):
        over_core(j).wait_send()
        if j:
            for k in range(n_tensor):
                over_plane(j, k).wait_send()
    for k in range(1, n_tensor):
        over_line(k).wait_send()
        exchange(k).wait_send()


def project_kernel(ids_ref, x_ref, w_ref, out_ref, acc_ref, *, cols):
    owners, slots = ids_ref.shape[0], ids_ref.shape[2]
    tile = w_ref.shape[-1]
    t = pl.program_id(0)
    acc_ref[...] = jnp.zeros_like(acc_ref)

    def owner_step(owner, carry):
        parts = []
        for s in range(slots):
            block = ids_ref[owner, t, s]
            left = x_ref[:, lanes(block // cols, tile)]
            parts.append(jnp.dot(left, w_ref[owner, 0, s * tile:(s + 1) * tile, :], preferred_element_type=jnp.float32))
        for s in range(slots):
            place = lanes(ids_ref[owner, t, s] % cols, tile)
            acc_ref[:, place] += parts[s]
        return carry

    lax.fori_loop(0, owners, owner_step, 0)
    out_ref[0] = acc_ref[...].astype(out_ref.dtype)


def gradient_kernel(
    ids_ref, xt_ref, w_ref, g_ref, h_ref, inv_ref, gain_ref,
    tiles_ref, hgrad_ref, gpart_ref, acc_ref, *, cols,
):
    owners, slots = ids_ref.shape[0], ids_ref.shape[2]
    tile = w_ref.shape[-1]
    tokens, width = acc_ref.shape
    t = pl.program_id(0)

    @pl.when(t == 0)
    def _():
        acc_ref[...] = jnp.zeros_like(acc_ref)

    def owner_step(owner, carry):
        parts = []
        for s in range(slots):
            block = ids_ref[owner, t, s]
            g = g_ref[0, :, lanes(block % cols, tile)]
            parts.append(
                lax.dot_general(
                    g, w_ref[owner, 0, s * tile:(s + 1) * tile, :], (((1,), (1,)), ((), ())),
                    preferred_element_type=jnp.float32,
                )
            )
            left = xt_ref[lanes(block // cols, tile), :]
            tiles_ref[owner, 0, s * tile:(s + 1) * tile, :] = jnp.dot(left, g, preferred_element_type=jnp.float32).astype(
                tiles_ref.dtype
            )
        for s in range(slots):
            place = lanes(ids_ref[owner, t, s] // cols, tile)
            acc_ref[:, place] += parts[s]
        return carry

    lax.fori_loop(0, owners, owner_step, 0)

    @pl.when(t == pl.num_programs(0) - 1)
    def _():
        rows = 16
        gpart_ref[...] = jnp.zeros_like(gpart_ref)

        def row_step(i, carry):
            at = pl.ds(pl.multiple_of(i * rows, rows), rows)
            inverse = inv_ref[at, :]
            unit = h_ref[at, :].astype(jnp.float32) * inverse
            row_grad = acc_ref[at, :]
            product = row_grad * unit
            gpart_ref[...] += jnp.sum(product, axis=0, keepdims=True)
            mean = jnp.mean(product * gain_ref[...], axis=-1, keepdims=True)
            hgrad_ref[at, :] = (
                inverse * (row_grad * gain_ref[...] - unit * mean)
            ).astype(hgrad_ref.dtype)
            return carry

        lax.fori_loop(0, tokens // rows, row_step, 0)


def body(hidden, norm_gain, tile_values, tile_ids, tile_counts, proj_grad):
    tokens, width = hidden.shape
    _, slots, tile, _ = tile_values.shape
    seq, part_cols = proj_grad.shape
    cols = part_cols // tile
    n_tensor = lax.axis_size("tensor")
    n_dp = lax.axis_size("dp")
    live = jnp.arange(slots) < tile_counts[0, 0]
    masked = jnp.where(live[:, None, None], tile_values[0], 0)

    pairs = n_dp // 2
    rows = slots * tile
    numbers = jnp.stack([tile_ids[0] // cols, tile_ids[0] % cols]).astype(jnp.bfloat16)
    numbers = jnp.pad(numbers, ((0, TAIL - 2), (0, tile - slots)))
    packed = jnp.concatenate([masked.reshape(rows, tile), numbers], axis=0)
    dma = pltpu.SemaphoreType.DMA
    in_hbm = pl.BlockSpec(memory_space=pl.ANY)
    in_vmem = pl.BlockSpec(memory_space=pltpu.VMEM)
    weights, grads, normed, flipped, inverse = pl.pallas_call(
        functools.partial(spread_kernel, pairs=pairs, n_tensor=n_tensor, tile=tile),
        out_shape=(
            jax.ShapeDtypeStruct((n_dp, n_tensor, rows + TAIL, tile), jnp.bfloat16),
            jax.ShapeDtypeStruct((n_tensor, tokens, part_cols), jnp.bfloat16),
            jax.ShapeDtypeStruct((tokens, width), jnp.bfloat16),
            jax.ShapeDtypeStruct((width, tokens), jnp.bfloat16),
            jax.ShapeDtypeStruct((tokens, 1), jnp.float32),
        ),
        in_specs=[in_hbm, in_hbm, in_vmem, in_vmem],
        out_specs=[in_hbm, in_hbm, in_vmem, in_vmem, in_vmem],
        scratch_shapes=[
            dma((n_tensor,)), dma((n_tensor,)),
            dma((n_tensor, pairs)), dma((n_tensor, pairs)),
            dma((n_tensor, pairs)), dma((n_tensor, pairs)),
            dma((n_tensor,)), dma((n_tensor,)), dma((2,)),
        ],
        compiler_params=pltpu.CompilerParams(
            collective_id=0, has_side_effects=True, vmem_limit_bytes=VMEM_BYTES
        ),
        name="spread",
    )(packed, proj_grad.reshape(n_tensor, tokens, part_cols), hidden, norm_gain[None, :])
    numbers = weights[:, :, rows:rows + 2, :slots].astype(jnp.int32)
    ids = numbers[:, :, 0] * cols + numbers[:, :, 1]

    whole = lambda *shape: pl.BlockSpec(shape, lambda t, ids: (0,) * len(shape))
    w_spec = pl.BlockSpec((n_dp, 1, rows + TAIL, tile), lambda t, ids: (0, t, 0, 0))
    t_spec = pl.BlockSpec((n_dp, 1, rows, tile), lambda t, ids: (0, t, 0, 0))
    c_spec = pl.BlockSpec((1, tokens, part_cols), lambda t, ids: (t, 0, 0))
    total = n_dp * n_tensor * slots
    flops = 2 * total * tokens * tile * tile
    params = pltpu.CompilerParams(
        dimension_semantics=("arbitrary",), vmem_limit_bytes=VMEM_BYTES
    )
    projected = pl.pallas_call(
        functools.partial(project_kernel, cols=cols),
        out_shape=jax.ShapeDtypeStruct((n_tensor, tokens, part_cols), jnp.bfloat16),
        grid_spec=pltpu.PrefetchScalarGridSpec(
            num_scalar_prefetch=1,
            grid=(n_tensor,),
            in_specs=[whole(tokens, width), w_spec],
            out_specs=c_spec,
            scratch_shapes=[pltpu.VMEM((tokens, part_cols), jnp.float32)],
        ),
        compiler_params=params,
        cost_estimate=pl.CostEstimate(
            flops=4 * flops, bytes_accessed=2 * total * tile * tile, transcendentals=0
        ),
        name="project",
    )(ids, normed, weights)
    tile_parts, hidden_grad, gain_part = pl.pallas_call(
        functools.partial(gradient_kernel, cols=cols),
        out_shape=(
            jax.ShapeDtypeStruct((n_dp, n_tensor, rows, tile), jnp.bfloat16),
            jax.ShapeDtypeStruct((tokens, width), jnp.bfloat16),
            jax.ShapeDtypeStruct((1, width), jnp.float32),
        ),
        grid_spec=pltpu.PrefetchScalarGridSpec(
            num_scalar_prefetch=1,
            grid=(n_tensor,),
            in_specs=[
                whole(width, tokens), w_spec, c_spec, whole(tokens, width),
                whole(tokens, 1), whole(1, width),
            ],
            out_specs=[t_spec, whole(tokens, width), whole(1, width)],
            scratch_shapes=[pltpu.VMEM((tokens, width), jnp.float32)],
        ),
        compiler_params=params,
        cost_estimate=pl.CostEstimate(
            flops=8 * flops, bytes_accessed=4 * total * tile * tile, transcendentals=0
        ),
        name="gradient",
    )(ids, flipped, weights, grads, hidden, inverse, norm_gain[None, :])

    chunk = (n_tensor, rows, tile)
    held = 2 * (3 * pairs + 1) * n_tensor * rows * tile
    if held < VMEM_BYTES // 2:
        small = (8, width // 8)
        f32 = jnp.float32
        tile_sum, projections, gain_grad = pl.pallas_call(
            functools.partial(collect_kernel, pairs=pairs, n_tensor=n_tensor, tile=tile),
            out_shape=(
                jax.ShapeDtypeStruct((rows, tile), f32),
                jax.ShapeDtypeStruct((n_tensor, tokens, part_cols), jnp.bfloat16),
                jax.ShapeDtypeStruct(small, f32),
            ),
            in_specs=[in_hbm, in_hbm, in_vmem],
            out_specs=[in_vmem, in_hbm, in_vmem],
            scratch_shapes=[
                pltpu.VMEM((pairs,) + chunk, jnp.bfloat16),
                pltpu.VMEM((pairs,) + chunk, jnp.bfloat16),
                pltpu.VMEM((pairs,) + chunk, jnp.bfloat16),
                pltpu.VMEM(chunk, jnp.bfloat16),
                pltpu.VMEM(small, f32),
                pltpu.VMEM((pairs,) + small, f32),
                pltpu.VMEM((n_tensor,) + small, f32),
                dma((pairs,)), dma((pairs,)),
                dma((pairs, n_tensor)), dma((pairs, n_tensor)),
                dma((n_tensor,)), dma((n_tensor,)), dma((n_tensor,)), dma((n_tensor,)),
                dma, dma, dma((pairs,)), dma((pairs,)), dma((n_tensor,)), dma((n_tensor,)),
                dma((pairs,)), dma,
            ],
            compiler_params=pltpu.CompilerParams(
                collective_id=1, has_side_effects=True, vmem_limit_bytes=VMEM_BYTES
            ),
            name="collect",
        )(tile_parts, projected, gain_part.reshape(small))
        gain_grad = gain_grad.reshape(width)
    else:
        projections = lax.all_to_all(projected, "tensor", split_axis=0, concat_axis=0)
        plane = lax.psum_scatter(tile_parts, "dp", scatter_dimension=0, tiled=False)
        tile_sum = lax.psum_scatter(plane, "tensor", scatter_dimension=0, tiled=False)
        gain_grad = lax.psum(gain_part[0], ("dp", "tensor"))
    projections = projections.reshape(seq, part_cols)
    tile_sum = tile_sum.reshape(slots, tile, tile).astype(jnp.float32)
    tile_grads = jnp.where(live[:, None, None], tile_sum, 0.0)[None]
    return (projections, hidden_grad, tile_grads, gain_grad)


def solution(mesh):
    in_specs = (
        P(("dp", "tensor"), None),
        P(),
        P("tensor", "dp", None, None),
        P("tensor", "dp"),
        P("tensor", "dp"),
        P("dp", "tensor"),
    )
    out_specs = (P("dp", "tensor"), P(("dp", "tensor"), None), P("tensor", "dp", None, None), P())
    return jax.shard_map(body, mesh=mesh, in_specs=in_specs, out_specs=out_specs, check_vma=False)
```

```python
import functools

import jax
import jax.numpy as jnp
from jax import lax
from jax.experimental import pallas as pl
from jax.experimental.pallas import tpu as pltpu
from jax.sharding import PartitionSpec as P

EPSILON = 1e-05
VMEM_BYTES = 56 * 1024 * 1024
MESH = pl.DeviceIdType.MESH
TAIL = 16


def lanes(block, tile):
    return pl.ds(pl.multiple_of(block * tile, tile), tile)


def spread_kernel(
    tiles_ref, g_ref, h_ref, gain_ref,
    w_ref, grads_ref, x_ref, xt_ref, inv_ref, tail_ref,
    up_send, down_send, z_recv, p_send, p_recv, c_send, c_recv, a_send, a_recv, l_sem,
    *, pairs, n_tensor, tile,
):
    d = lax.axis_index("dp")
    t = lax.axis_index("tensor")
    core = lax.rem(d, 2)
    pair = d // 2
    other = pair * 2 + 1 - core

    def line(k):
        return lax.rem(t + k + n_tensor, n_tensor)

    def peer(j):
        return lax.rem(pair + j + pairs, pairs) * 2 + core

    greet(d, t, other, peer, line, pairs, n_tensor)

    def remote(src, dst, send, recv, to):
        return pltpu.make_async_remote_copy(
            src_ref=src, dst_ref=dst, send_sem=send, recv_sem=recv,
            device_id=to, device_id_type=MESH,
        )

    def hop(q, step, src):
        send = up_send if step > 0 else down_send
        return remote(src, w_ref.at[d, q], send.at[q], z_recv.at[q], (d, t + step))

    def over_plane(q, j, src):
        return remote(src, w_ref.at[d, q], p_send.at[q, j], p_recv.at[q, j], (peer(j), t))

    def over_core(q, j, src):
        slot = w_ref.at[peer(-j), q]
        return remote(src, slot, c_send.at[q, j], c_recv.at[q, j], (other, t))

    def exchange(k):
        return remote(
            g_ref.at[line(k)], grads_ref.at[t], a_send.at[k], a_recv.at[k], (d, line(k))
        )

    def landed(slot, send, recv):
        remote(slot, slot, send, recv, (other, t)).wait_recv()

    def share(q, src):
        for j in range(1, pairs):
            over_plane(q, j, src).start()
        over_core(q, 0, src).start()

    @pl.when(t + 1 < n_tensor)
    def _():
        hop(t, 1, tiles_ref).start()

    @pl.when(t > 0)
    def _():
        hop(t, -1, tiles_ref).start()

    share(t, tiles_ref)
    own = (
        pltpu.make_async_copy(tiles_ref, w_ref.at[d, t], l_sem.at[0]),
        pltpu.make_async_copy(g_ref.at[t], grads_ref.at[t], l_sem.at[1]),
    )
    for copy in own:
        copy.start()

    tokens, width = h_ref.shape
    rows = 16

    def norm_step(i, carry):
        at = pl.ds(pl.multiple_of(i * rows, rows), rows)
        hidden = h_ref[at, :].astype(jnp.float32)
        inverse = lax.rsqrt(jnp.mean(hidden * hidden, axis=-1, keepdims=True) + EPSILON)
        inv_ref[at, :] = inverse
        x_ref[at, :] = (hidden * inverse * gain_ref[...]).astype(x_ref.dtype)
        return carry

    lax.fori_loop(0, tokens // rows, norm_step, 0)

    for far in range(1, n_tensor):
        for step in (1, -1):
            q = t - step * far
            ends = (q >= 0) if step > 0 else (q < n_tensor)
            more = (t + 1 < n_tensor) if step > 0 else (t > 0)

            @pl.when(ends)
            def _(q=q, step=step, more=more):
                slot = w_ref.at[d, q]
                landed(slot, p_send.at[q, 0], z_recv.at[q])

                @pl.when(more)
                def _():
                    hop(q, step, slot).start()

                share(q, slot)

    for k in range(1, n_tensor):
        exchange(k).start()

    def flip_step(i, carry):
        at = lanes(i, tile)
        xt_ref[at, :] = x_ref[:, at].astype(jnp.float32).T.astype(xt_ref.dtype)
        return carry

    lax.fori_loop(0, width // tile, flip_step, 0)

    for k in range(n_tensor):
        q = line(-k)
        for j in range(1, pairs):
            slot = w_ref.at[peer(-j), q]
            landed(slot, p_send.at[q, j], p_recv.at[q, j])
            over_core(q, j, slot).start()
    for k in range(n_tensor):
        q = line(-k)
        for j in range(pairs):
            far = lax.rem(pair - j + pairs, pairs) * 2 + 1 - core
            landed(w_ref.at[far, q], c_send.at[q, j], c_recv.at[q, j])
    for copy in own:
        copy.wait()
    tails = pltpu.make_async_copy(
        w_ref.at[:, :, pl.ds(w_ref.shape[2] - TAIL, TAIL), :], tail_ref, l_sem.at[2]
    )
    tails.start()
    for k in range(1, n_tensor):
        landed(grads_ref.at[line(-k)], a_send.at[k], a_recv.at[k])
    tails.wait()
    for q in range(n_tensor):

        @pl.when((q <= t) & (t + 1 < n_tensor))
        def _(q=q):
            hop(q, 1, w_ref.at[d, q]).wait_send()

        @pl.when((q >= t) & (t > 0))
        def _(q=q):
            hop(q, -1, w_ref.at[d, q]).wait_send()

        if q:
            exchange(q).wait_send()
        for j in range(pairs):
            if j:
                over_plane(q, j, w_ref.at[d, q]).wait_send()
            over_core(q, j, w_ref.at[peer(-j), q]).wait_send()


def greet(d, t, other, peer, line, pairs, n_tensor):
    barrier = pltpu.get_barrier_semaphore()
    targets = [(other, t)]
    targets += [(peer(j), t) for j in range(1, pairs)]
    targets += [(d, line(k)) for k in range(1, n_tensor)]
    for target in targets:
        pl.semaphore_signal(barrier, inc=1, device_id=target, device_id_type=MESH)
    pl.semaphore_wait(barrier, len(targets))


def collect_kernel(
    parts_ref, gain_ref, sum_ref, total_ref,
    mine, from_core, from_plane, from_line, g_core, g_plane, g_line,
    c_send, c_recv, p_send, p_recv, z_send, z_recv,
    gc_send, gc_recv, gp_send, gp_recv, gz_send, gz_recv, l_sem,
    *, pairs, n_tensor, tile,
):
    d = lax.axis_index("dp")
    t = lax.axis_index("tensor")
    core = lax.rem(d, 2)
    pair = d // 2
    other = pair * 2 + 1 - core

    def line(k):
        return lax.rem(t + k + n_tensor, n_tensor)

    def near(j):
        return lax.rem(pair + j + pairs, pairs)

    def peer(j):
        return near(j) * 2 + core

    greet(d, t, other, peer, line, pairs, n_tensor)

    def remote(src, dst, send, recv, to):
        return pltpu.make_async_remote_copy(
            src_ref=src, dst_ref=dst, send_sem=send, recv_sem=recv,
            device_id=to, device_id_type=MESH,
        )

    def over_core(j):
        return remote(
            parts_ref.at[near(j) * 2 + 1 - core], from_core.at[near(j)],
            c_send.at[j], c_recv.at[j], (other, t),
        )

    def load_own(j):
        return pltpu.make_async_copy(parts_ref.at[peer(j)], mine.at[near(j)], l_sem.at[j])

    def over_plane(j, k):
        return remote(
            mine.at[near(j), line(k)], from_plane.at[pair, line(k)],
            p_send.at[j, k], p_recv.at[j, k], (peer(j), t),
        )

    def over_line(k):
        return remote(
            mine.at[pair, line(k)], from_line.at[k], z_send.at[k], z_recv.at[k], (d, line(k))
        )

    def landed(slot, send, recv):
        remote(slot, slot, send, recv, (other, t)).wait_recv()

    order = list(range(1, pairs)) + [0]
    gain_core = remote(gain_ref, g_core, gc_send, gc_recv, (other, t))
    gain_core.start()
    for j in order:
        over_core(j).start()
        load_own(j).start()

    gain_core.wait_recv()
    g_plane[pair] = gain_ref[...] + g_core[...]
    gain_plane = [
        remote(g_plane.at[pair], g_plane.at[pair], gp_send.at[j], gp_recv.at[j], (peer(j), t))
        for j in range(1, pairs)
    ]
    for copy in gain_plane:
        copy.start()

    steps = mine.shape[2] // tile
    f32 = jnp.float32
    lines = list(range(1, n_tensor)) + [0]
    for j in range(1, pairs):
        load_own(j).wait()
        landed(from_core.at[near(j)], c_send.at[j], c_recv.at[j])
        for k in lines:

            def core_step(i, carry, j=j, k=k):
                at = lanes(i, tile)
                both = mine[near(j), line(k), at, :].astype(f32)
                both += from_core[near(j), line(k), at, :].astype(f32)
                mine[near(j), line(k), at, :] = both.astype(mine.dtype)
                return carry

            lax.fori_loop(0, steps, core_step, 0)
            over_plane(j, k).start()
    load_own(0).wait()
    landed(from_core.at[pair], c_send.at[0], c_recv.at[0])

    for j in range(1, pairs):
        landed(g_plane.at[near(-j)], gp_send.at[j], gp_recv.at[j])
    whole_plane = g_plane[0]
    for p in range(1, pairs):
        whole_plane += g_plane[p]
    g_line[t] = whole_plane
    gain_line = [
        remote(g_line.at[t], g_line.at[t], gz_send.at[k], gz_recv.at[k], (d, line(k)))
        for k in range(1, n_tensor)
    ]
    for copy in gain_line:
        copy.start()

    for k in lines:
        for j in range(1, pairs):
            landed(from_plane.at[near(-j), line(k)], p_send.at[j, k], p_recv.at[j, k])

        def plane_step(i, carry, k=k):
            at = lanes(i, tile)
            total = mine[pair, line(k), at, :].astype(f32)
            total += from_core[pair, line(k), at, :].astype(f32)
            for j in range(1, pairs):
                total += from_plane[near(-j), line(k), at, :].astype(f32)
            if k:
                mine[pair, line(k), at, :] = total.astype(mine.dtype)
            else:
                sum_ref[at, :] = total
            return carry

        lax.fori_loop(0, steps, plane_step, 0)
        if k:
            over_line(k).start()

    for k in range(1, n_tensor):
        landed(g_line.at[line(-k)], gz_send.at[k], gz_recv.at[k])
    whole_line = g_line[0]
    for q in range(1, n_tensor):
        whole_line += g_line[q]
    total_ref[...] = whole_line

    for k in range(1, n_tensor):
        landed(from_line.at[k], z_send.at[k], z_recv.at[k])

    def line_step(i, carry):
        at = lanes(i, tile)
        total = sum_ref[at, :]
        for k in range(1, n_tensor):
            total += from_line[k, at, :].astype(f32)
        sum_ref[at, :] = total
        return carry

    lax.fori_loop(0, steps, line_step, 0)

    gain_core.wait_send()
    for copy in gain_plane + gain_line:
        copy.wait_send()
    for j in range(pairs):
        over_core(j).wait_send()
        if j:
            for k in range(n_tensor):
                over_plane(j, k).wait_send()
    for k in range(1, n_tensor):
        over_line(k).wait_send()


def project_kernel(ids_ref, x_ref, w_ref, out_ref, acc_ref, *, cols):
    owners, slots = ids_ref.shape[0], ids_ref.shape[2]
    tile = w_ref.shape[-1]
    t = pl.program_id(0)
    acc_ref[...] = jnp.zeros_like(acc_ref)

    def owner_step(owner, carry):
        parts = []
        for s in range(slots):
            block = ids_ref[owner, t, s]
            left = x_ref[:, lanes(block // cols, tile)]
            parts.append(jnp.dot(left, w_ref[owner, 0, s * tile:(s + 1) * tile, :], preferred_element_type=jnp.float32))
        for s in range(slots):
            place = lanes(ids_ref[owner, t, s] % cols, tile)
            acc_ref[:, place] += parts[s]
        return carry

    lax.fori_loop(0, owners, owner_step, 0)
    out_ref[0] = acc_ref[...].astype(out_ref.dtype)


def gradient_kernel(
    ids_ref, xt_ref, w_ref, g_ref, h_ref, inv_ref, gain_ref,
    tiles_ref, hgrad_ref, gpart_ref, acc_ref, *, cols,
):
    owners, slots = ids_ref.shape[0], ids_ref.shape[2]
    tile = w_ref.shape[-1]
    tokens, width = acc_ref.shape
    t = pl.program_id(0)

    @pl.when(t == 0)
    def _():
        acc_ref[...] = jnp.zeros_like(acc_ref)

    def owner_step(owner, carry):
        parts = []
        for s in range(slots):
            block = ids_ref[owner, t, s]
            g = g_ref[0, :, lanes(block % cols, tile)]
            parts.append(
                lax.dot_general(
                    g, w_ref[owner, 0, s * tile:(s + 1) * tile, :], (((1,), (1,)), ((), ())),
                    preferred_element_type=jnp.float32,
                )
            )
            left = xt_ref[lanes(block // cols, tile), :]
            tiles_ref[owner, 0, s * tile:(s + 1) * tile, :] = jnp.dot(left, g, preferred_element_type=jnp.float32).astype(
                tiles_ref.dtype
            )
        for s in range(slots):
            place = lanes(ids_ref[owner, t, s] // cols, tile)
            acc_ref[:, place] += parts[s]
        return carry

    lax.fori_loop(0, owners, owner_step, 0)

    @pl.when(t == pl.num_programs(0) - 1)
    def _():
        rows = 16
        gpart_ref[...] = jnp.zeros_like(gpart_ref)

        def row_step(i, carry):
            at = pl.ds(pl.multiple_of(i * rows, rows), rows)
            inverse = inv_ref[at, :]
            unit = h_ref[at, :].astype(jnp.float32) * inverse
            row_grad = acc_ref[at, :]
            product = row_grad * unit
            gpart_ref[...] += jnp.sum(product, axis=0, keepdims=True)
            mean = jnp.mean(product * gain_ref[...], axis=-1, keepdims=True)
            hgrad_ref[at, :] = (
                inverse * (row_grad * gain_ref[...] - unit * mean)
            ).astype(hgrad_ref.dtype)
            return carry

        lax.fori_loop(0, tokens // rows, row_step, 0)


def body(hidden, norm_gain, tile_values, tile_ids, tile_counts, proj_grad):
    tokens, width = hidden.shape
    _, slots, tile, _ = tile_values.shape
    seq, part_cols = proj_grad.shape
    cols = part_cols // tile
    n_tensor = lax.axis_size("tensor")
    n_dp = lax.axis_size("dp")
    live = jnp.arange(slots) < tile_counts[0, 0]
    masked = jnp.where(live[:, None, None], tile_values[0], 0)

    pairs = n_dp // 2
    rows = slots * tile
    numbers = jnp.stack([tile_ids[0] // cols, tile_ids[0] % cols]).astype(jnp.bfloat16)
    numbers = jnp.pad(numbers, ((0, TAIL - 2), (0, tile - slots)))
    packed = jnp.concatenate([masked.reshape(rows, tile), numbers], axis=0)
    dma = pltpu.SemaphoreType.DMA
    in_hbm = pl.BlockSpec(memory_space=pl.ANY)
    in_vmem = pl.BlockSpec(memory_space=pltpu.VMEM)
    weights, grads, normed, flipped, inverse, tails = pl.pallas_call(
        functools.partial(spread_kernel, pairs=pairs, n_tensor=n_tensor, tile=tile),
        out_shape=(
            jax.ShapeDtypeStruct((n_dp, n_tensor, rows + TAIL, tile), jnp.bfloat16),
            jax.ShapeDtypeStruct((n_tensor, tokens, part_cols), jnp.bfloat16),
            jax.ShapeDtypeStruct((tokens, width), jnp.bfloat16),
            jax.ShapeDtypeStruct((width, tokens), jnp.bfloat16),
            jax.ShapeDtypeStruct((tokens, 1), jnp.float32),
            jax.ShapeDtypeStruct((n_dp, n_tensor, TAIL, tile), jnp.bfloat16),
        ),
        in_specs=[in_hbm, in_hbm, in_vmem, in_vmem],
        out_specs=[in_hbm, in_hbm, in_vmem, in_vmem, in_vmem, in_vmem],
        scratch_shapes=[
            dma((n_tensor,)), dma((n_tensor,)), dma((n_tensor,)),
            dma((n_tensor, pairs)), dma((n_tensor, pairs)),
            dma((n_tensor, pairs)), dma((n_tensor, pairs)),
            dma((n_tensor,)), dma((n_tensor,)), dma((3,)),
        ],
        compiler_params=pltpu.CompilerParams(
            collective_id=0, has_side_effects=True, vmem_limit_bytes=VMEM_BYTES
        ),
        name="spread",
    )(packed, proj_grad.reshape(n_tensor, tokens, part_cols), hidden, norm_gain[None, :])
    numbers = tails[:, :, :2, :slots].astype(jnp.int32)
    ids = numbers[:, :, 0] * cols + numbers[:, :, 1]

    whole = lambda *shape: pl.BlockSpec(shape, lambda t, ids: (0,) * len(shape))
    w_spec = pl.BlockSpec((n_dp, 1, rows + TAIL, tile), lambda t, ids: (0, t, 0, 0))
    t_spec = pl.BlockSpec((n_dp, 1, rows, tile), lambda t, ids: (0, t, 0, 0))
    c_spec = pl.BlockSpec((1, tokens, part_cols), lambda t, ids: (t, 0, 0))
    total = n_dp * n_tensor * slots
    flops = 2 * total * tokens * tile * tile
    params = pltpu.CompilerParams(
        dimension_semantics=("arbitrary",), vmem_limit_bytes=VMEM_BYTES
    )
    projected = pl.pallas_call(
        functools.partial(project_kernel, cols=cols),
        out_shape=jax.ShapeDtypeStruct((n_tensor, tokens, part_cols), jnp.bfloat16),
        grid_spec=pltpu.PrefetchScalarGridSpec(
            num_scalar_prefetch=1,
            grid=(n_tensor,),
            in_specs=[whole(tokens, width), w_spec],
            out_specs=c_spec,
            scratch_shapes=[pltpu.VMEM((tokens, part_cols), jnp.float32)],
        ),
        compiler_params=params,
        cost_estimate=pl.CostEstimate(
            flops=4 * flops, bytes_accessed=2 * total * tile * tile, transcendentals=0
        ),
        name="project",
    )(ids, normed, weights)
    projected, grads = lax.optimization_barrier((projected, grads))
    projections = lax.all_to_all(projected, "tensor", split_axis=0, concat_axis=0)
    tile_parts, hidden_grad, gain_part = pl.pallas_call(
        functools.partial(gradient_kernel, cols=cols),
        out_shape=(
            jax.ShapeDtypeStruct((n_dp, n_tensor, rows, tile), jnp.bfloat16),
            jax.ShapeDtypeStruct((tokens, width), jnp.bfloat16),
            jax.ShapeDtypeStruct((1, width), jnp.float32),
        ),
        grid_spec=pltpu.PrefetchScalarGridSpec(
            num_scalar_prefetch=1,
            grid=(n_tensor,),
            in_specs=[
                whole(width, tokens), w_spec, c_spec, whole(tokens, width),
                whole(tokens, 1), whole(1, width),
            ],
            out_specs=[t_spec, whole(tokens, width), whole(1, width)],
            scratch_shapes=[pltpu.VMEM((tokens, width), jnp.float32)],
        ),
        compiler_params=params,
        cost_estimate=pl.CostEstimate(
            flops=8 * flops, bytes_accessed=4 * total * tile * tile, transcendentals=0
        ),
        name="gradient",
    )(ids, flipped, weights, grads, hidden, inverse, norm_gain[None, :])

    chunk = (n_tensor, rows, tile)
    held = 2 * (3 * pairs + 1) * n_tensor * rows * tile
    if held < VMEM_BYTES // 2:
        small = (8, width // 8)
        f32 = jnp.float32
        tile_sum, gain_grad = pl.pallas_call(
            functools.partial(collect_kernel, pairs=pairs, n_tensor=n_tensor, tile=tile),
            out_shape=(
                jax.ShapeDtypeStruct((rows, tile), f32),
                jax.ShapeDtypeStruct(small, f32),
            ),
            in_specs=[in_hbm, in_vmem],
            out_specs=[in_vmem, in_vmem],
            scratch_shapes=[
                pltpu.VMEM((pairs,) + chunk, jnp.bfloat16),
                pltpu.VMEM((pairs,) + chunk, jnp.bfloat16),
                pltpu.VMEM((pairs,) + chunk, jnp.bfloat16),
                pltpu.VMEM(chunk, jnp.bfloat16),
                pltpu.VMEM(small, f32),
                pltpu.VMEM((pairs,) + small, f32),
                pltpu.VMEM((n_tensor,) + small, f32),
                dma((pairs,)), dma((pairs,)),
                dma((pairs, n_tensor)), dma((pairs, n_tensor)),
                dma((n_tensor,)), dma((n_tensor,)),
                dma, dma, dma((pairs,)), dma((pairs,)), dma((n_tensor,)), dma((n_tensor,)),
                dma((pairs,)),
            ],
            compiler_params=pltpu.CompilerParams(
                collective_id=1, has_side_effects=True, vmem_limit_bytes=VMEM_BYTES
            ),
            name="collect",
        )(tile_parts, gain_part.reshape(small))
        gain_grad = gain_grad.reshape(width)
    else:
        plane = lax.psum_scatter(tile_parts, "dp", scatter_dimension=0, tiled=False)
        tile_sum = lax.psum_scatter(plane, "tensor", scatter_dimension=0, tiled=False)
        gain_grad = lax.psum(gain_part[0], ("dp", "tensor"))
    projections = projections.reshape(seq, part_cols)
    tile_sum = tile_sum.reshape(slots, tile, tile).astype(jnp.float32)
    tile_grads = jnp.where(live[:, None, None], tile_sum, 0.0)[None]
    return (projections, hidden_grad, tile_grads, gain_grad)


def solution(mesh):
    in_specs = (
        P(("dp", "tensor"), None),
        P(),
        P("tensor", "dp", None, None),
        P("tensor", "dp"),
        P("tensor", "dp"),
        P("dp", "tensor"),
    )
    out_specs = (P("dp", "tensor"), P(("dp", "tensor"), None), P("tensor", "dp", None, None), P())
    return jax.shard_map(body, mesh=mesh, in_specs=in_specs, out_specs=out_specs, check_vma=False)
```

```python
import functools

import jax
import jax.numpy as jnp
from jax import lax
from jax.experimental import pallas as pl
from jax.experimental.pallas import tpu as pltpu
from jax.sharding import PartitionSpec as P

EPSILON = 1e-05
VMEM_BYTES = 56 * 1024 * 1024
MESH = pl.DeviceIdType.MESH
TAIL = 16


def lanes(block, tile):
    return pl.ds(pl.multiple_of(block * tile, tile), tile)


def spread_kernel(
    tiles_ref, g_ref, h_ref, gain_ref,
    w_ref, grads_ref, x_ref, xt_ref, inv_ref, tail_ref,
    up_send, down_send, z_recv, p_send, p_recv, c_send, c_recv, a_send, a_recv, l_sem,
    *, pairs, n_tensor, tile,
):
    d = lax.axis_index("dp")
    t = lax.axis_index("tensor")
    core = lax.rem(d, 2)
    pair = d // 2
    other = pair * 2 + 1 - core

    def line(k):
        return lax.rem(t + k + n_tensor, n_tensor)

    def peer(j):
        return lax.rem(pair + j + pairs, pairs) * 2 + core

    greet(d, t, other, peer, line, pairs, n_tensor)

    def remote(src, dst, send, recv, to):
        return pltpu.make_async_remote_copy(
            src_ref=src, dst_ref=dst, send_sem=send, recv_sem=recv,
            device_id=to, device_id_type=MESH,
        )

    def hop(q, step, src):
        send = up_send if step > 0 else down_send
        return remote(src, w_ref.at[d, q], send.at[q], z_recv.at[q], (d, t + step))

    def over_plane(q, j, src):
        return remote(src, w_ref.at[d, q], p_send.at[q, j], p_recv.at[q, j], (peer(j), t))

    def over_core(q, j, src):
        slot = w_ref.at[peer(-j), q]
        return remote(src, slot, c_send.at[q, j], c_recv.at[q, j], (other, t))

    def exchange(k):
        return remote(
            g_ref.at[line(k)], grads_ref.at[t], a_send.at[k], a_recv.at[k], (d, line(k))
        )

    def landed(slot, send, recv):
        remote(slot, slot, send, recv, (other, t)).wait_recv()

    def share(q, src):
        for j in range(1, pairs):
            over_plane(q, j, src).start()
        over_core(q, 0, src).start()

    @pl.when(t + 1 < n_tensor)
    def _():
        hop(t, 1, tiles_ref).start()

    @pl.when(t > 0)
    def _():
        hop(t, -1, tiles_ref).start()

    share(t, tiles_ref)
    own = (
        pltpu.make_async_copy(tiles_ref, w_ref.at[d, t], l_sem.at[0]),
        pltpu.make_async_copy(g_ref.at[t], grads_ref.at[t], l_sem.at[1]),
    )
    for copy in own:
        copy.start()

    tokens, width = h_ref.shape
    rows = 16

    def norm_step(i, carry):
        at = pl.ds(pl.multiple_of(i * rows, rows), rows)
        hidden = h_ref[at, :].astype(jnp.float32)
        inverse = lax.rsqrt(jnp.mean(hidden * hidden, axis=-1, keepdims=True) + EPSILON)
        inv_ref[at, :] = inverse
        x_ref[at, :] = (hidden * inverse * gain_ref[...]).astype(x_ref.dtype)
        return carry

    lax.fori_loop(0, tokens // rows, norm_step, 0)

    for far in range(1, n_tensor):
        for step in (1, -1):
            q = t - step * far
            ends = (q >= 0) if step > 0 else (q < n_tensor)
            more = (t + 1 < n_tensor) if step > 0 else (t > 0)

            @pl.when(ends)
            def _(q=q, step=step, more=more):
                slot = w_ref.at[d, q]
                landed(slot, p_send.at[q, 0], z_recv.at[q])

                @pl.when(more)
                def _():
                    hop(q, step, slot).start()

                share(q, slot)

        if far == 1:
            for k in range(1, n_tensor):
                exchange(k).start()

    def flip_step(i, carry):
        at = lanes(i, tile)
        xt_ref[at, :] = x_ref[:, at].astype(jnp.float32).T.astype(xt_ref.dtype)
        return carry

    lax.fori_loop(0, width // tile, flip_step, 0)

    for k in range(n_tensor):
        q = line(-k)
        for j in range(1, pairs):
            slot = w_ref.at[peer(-j), q]
            landed(slot, p_send.at[q, j], p_recv.at[q, j])
            over_core(q, j, slot).start()
    for k in range(n_tensor):
        q = line(-k)
        for j in range(pairs):
            far = lax.rem(pair - j + pairs, pairs) * 2 + 1 - core
            landed(w_ref.at[far, q], c_send.at[q, j], c_recv.at[q, j])
    for copy in own:
        copy.wait()
    tails = pltpu.make_async_copy(
        w_ref.at[:, :, pl.ds(w_ref.shape[2] - TAIL, TAIL), :], tail_ref, l_sem.at[2]
    )
    tails.start()
    for k in range(1, n_tensor):
        landed(grads_ref.at[line(-k)], a_send.at[k], a_recv.at[k])
    tails.wait()
    for q in range(n_tensor):

        @pl.when((q <= t) & (t + 1 < n_tensor))
        def _(q=q):
            hop(q, 1, w_ref.at[d, q]).wait_send()

        @pl.when((q >= t) & (t > 0))
        def _(q=q):
            hop(q, -1, w_ref.at[d, q]).wait_send()

        if q:
            exchange(q).wait_send()
        for j in range(pairs):
            if j:
                over_plane(q, j, w_ref.at[d, q]).wait_send()
            over_core(q, j, w_ref.at[peer(-j), q]).wait_send()


def greet(d, t, other, peer, line, pairs, n_tensor):
    barrier = pltpu.get_barrier_semaphore()
    targets = [(other, t)]
    targets += [(peer(j), t) for j in range(1, pairs)]
    targets += [(d, line(k)) for k in range(1, n_tensor)]
    for target in targets:
        pl.semaphore_signal(barrier, inc=1, device_id=target, device_id_type=MESH)
    pl.semaphore_wait(barrier, len(targets))


def collect_kernel(
    parts_ref, gain_ref, sum_ref, total_ref,
    mine, from_core, from_plane, from_line, g_core, g_plane, g_line,
    c_send, c_recv, p_send, p_recv, z_send, z_recv,
    gc_send, gc_recv, gp_send, gp_recv, gz_send, gz_recv, l_sem,
    *, pairs, n_tensor, tile,
):
    d = lax.axis_index("dp")
    t = lax.axis_index("tensor")
    core = lax.rem(d, 2)
    pair = d // 2
    other = pair * 2 + 1 - core

    def line(k):
        return lax.rem(t + k + n_tensor, n_tensor)

    def near(j):
        return lax.rem(pair + j + pairs, pairs)

    def peer(j):
        return near(j) * 2 + core

    greet(d, t, other, peer, line, pairs, n_tensor)

    def remote(src, dst, send, recv, to):
        return pltpu.make_async_remote_copy(
            src_ref=src, dst_ref=dst, send_sem=send, recv_sem=recv,
            device_id=to, device_id_type=MESH,
        )

    def over_core(j, k):
        return remote(
            parts_ref.at[near(j) * 2 + 1 - core, line(k)], from_core.at[near(j), line(k)],
            c_send.at[j, k], c_recv.at[j, k], (other, t),
        )

    def load_own(j, k):
        return pltpu.make_async_copy(
            parts_ref.at[peer(j), line(k)], mine.at[near(j), line(k)], l_sem.at[j, k]
        )

    def own_landed(j, k):
        load_own(j, k).wait()
        landed(from_core.at[near(j), line(k)], c_send.at[j, k], c_recv.at[j, k])

    def over_plane(j, k):
        return remote(
            mine.at[near(j), line(k)], from_plane.at[pair, line(k)],
            p_send.at[j, k], p_recv.at[j, k], (peer(j), t),
        )

    def over_line(k):
        return remote(
            mine.at[pair, line(k)], from_line.at[k], z_send.at[k], z_recv.at[k], (d, line(k))
        )

    def landed(slot, send, recv):
        remote(slot, slot, send, recv, (other, t)).wait_recv()

    order = list(range(1, pairs)) + [0]
    gain_core = remote(gain_ref, g_core, gc_send, gc_recv, (other, t))
    gain_core.start()
    lines = list(range(1, n_tensor)) + [0]
    for k in lines:
        for j in order:
            over_core(j, k).start()
            load_own(j, k).start()

    gain_core.wait_recv()
    g_plane[pair] = gain_ref[...] + g_core[...]
    gain_plane = [
        remote(g_plane.at[pair], g_plane.at[pair], gp_send.at[j], gp_recv.at[j], (peer(j), t))
        for j in range(1, pairs)
    ]
    for copy in gain_plane:
        copy.start()

    steps = mine.shape[2] // tile
    f32 = jnp.float32
    for k in lines:
        for j in range(1, pairs):
            own_landed(j, k)

            def core_step(i, carry, j=j, k=k):
                at = lanes(i, tile)
                both = mine[near(j), line(k), at, :].astype(f32)
                both += from_core[near(j), line(k), at, :].astype(f32)
                mine[near(j), line(k), at, :] = both.astype(mine.dtype)
                return carry

            lax.fori_loop(0, steps, core_step, 0)
            over_plane(j, k).start()

    for j in range(1, pairs):
        landed(g_plane.at[near(-j)], gp_send.at[j], gp_recv.at[j])
    whole_plane = g_plane[0]
    for p in range(1, pairs):
        whole_plane += g_plane[p]
    g_line[t] = whole_plane
    gain_line = [
        remote(g_line.at[t], g_line.at[t], gz_send.at[k], gz_recv.at[k], (d, line(k)))
        for k in range(1, n_tensor)
    ]
    for copy in gain_line:
        copy.start()

    for k in lines:
        own_landed(0, k)
        for j in range(1, pairs):
            landed(from_plane.at[near(-j), line(k)], p_send.at[j, k], p_recv.at[j, k])

        def plane_step(i, carry, k=k):
            at = lanes(i, tile)
            total = mine[pair, line(k), at, :].astype(f32)
            total += from_core[pair, line(k), at, :].astype(f32)
            for j in range(1, pairs):
                total += from_plane[near(-j), line(k), at, :].astype(f32)
            if k:
                mine[pair, line(k), at, :] = total.astype(mine.dtype)
            else:
                sum_ref[at, :] = total
            return carry

        lax.fori_loop(0, steps, plane_step, 0)
        if k:
            over_line(k).start()

    for k in range(1, n_tensor):
        landed(g_line.at[line(-k)], gz_send.at[k], gz_recv.at[k])
    whole_line = g_line[0]
    for q in range(1, n_tensor):
        whole_line += g_line[q]
    total_ref[...] = whole_line

    for k in range(1, n_tensor):
        landed(from_line.at[k], z_send.at[k], z_recv.at[k])

    def line_step(i, carry):
        at = lanes(i, tile)
        total = sum_ref[at, :]
        for k in range(1, n_tensor):
            total += from_line[k, at, :].astype(f32)
        sum_ref[at, :] = total
        return carry

    lax.fori_loop(0, steps, line_step, 0)

    gain_core.wait_send()
    for copy in gain_plane + gain_line:
        copy.wait_send()
    for j in range(pairs):
        for k in range(n_tensor):
            over_core(j, k).wait_send()
            if j:
                over_plane(j, k).wait_send()
    for k in range(1, n_tensor):
        over_line(k).wait_send()


def project_kernel(ids_ref, x_ref, w_ref, out_ref, acc_ref, *, cols):
    owners, slots = ids_ref.shape[0], ids_ref.shape[2]
    tile = w_ref.shape[-1]
    t = pl.program_id(0)
    acc_ref[...] = jnp.zeros_like(acc_ref)

    def owner_step(owner, carry):
        parts = []
        for s in range(slots):
            block = ids_ref[owner, t, s]
            left = x_ref[:, lanes(block // cols, tile)]
            parts.append(jnp.dot(left, w_ref[owner, 0, s * tile:(s + 1) * tile, :], preferred_element_type=jnp.float32))
        for s in range(slots):
            place = lanes(ids_ref[owner, t, s] % cols, tile)
            acc_ref[:, place] += parts[s]
        return carry

    lax.fori_loop(0, owners, owner_step, 0)
    out_ref[0] = acc_ref[...].astype(out_ref.dtype)


def gradient_kernel(
    ids_ref, xt_ref, w_ref, g_ref, h_ref, inv_ref, gain_ref,
    tiles_ref, hgrad_ref, gpart_ref, acc_ref, *, cols,
):
    owners, slots = ids_ref.shape[0], ids_ref.shape[2]
    tile = w_ref.shape[-1]
    tokens, width = acc_ref.shape
    t = pl.program_id(0)

    @pl.when(t == 0)
    def _():
        acc_ref[...] = jnp.zeros_like(acc_ref)

    def owner_step(owner, carry):
        parts = []
        for s in range(slots):
            block = ids_ref[owner, t, s]
            g = g_ref[0, :, lanes(block % cols, tile)]
            parts.append(
                lax.dot_general(
                    g, w_ref[owner, 0, s * tile:(s + 1) * tile, :], (((1,), (1,)), ((), ())),
                    preferred_element_type=jnp.float32,
                )
            )
            left = xt_ref[lanes(block // cols, tile), :]
            tiles_ref[owner, 0, s * tile:(s + 1) * tile, :] = jnp.dot(left, g, preferred_element_type=jnp.float32).astype(
                tiles_ref.dtype
            )
        for s in range(slots):
            place = lanes(ids_ref[owner, t, s] // cols, tile)
            acc_ref[:, place] += parts[s]
        return carry

    lax.fori_loop(0, owners, owner_step, 0)

    @pl.when(t == pl.num_programs(0) - 1)
    def _():
        rows = 16
        gpart_ref[...] = jnp.zeros_like(gpart_ref)

        def row_step(i, carry):
            at = pl.ds(pl.multiple_of(i * rows, rows), rows)
            inverse = inv_ref[at, :]
            unit = h_ref[at, :].astype(jnp.float32) * inverse
            row_grad = acc_ref[at, :]
            product = row_grad * unit
            gpart_ref[...] += jnp.sum(product, axis=0, keepdims=True)
            mean = jnp.mean(product * gain_ref[...], axis=-1, keepdims=True)
            hgrad_ref[at, :] = (
                inverse * (row_grad * gain_ref[...] - unit * mean)
            ).astype(hgrad_ref.dtype)
            return carry

        lax.fori_loop(0, tokens // rows, row_step, 0)


def body(hidden, norm_gain, tile_values, tile_ids, tile_counts, proj_grad):
    tokens, width = hidden.shape
    _, slots, tile, _ = tile_values.shape
    seq, part_cols = proj_grad.shape
    cols = part_cols // tile
    n_tensor = lax.axis_size("tensor")
    n_dp = lax.axis_size("dp")
    live = jnp.arange(slots) < tile_counts[0, 0]
    masked = jnp.where(live[:, None, None], tile_values[0], 0)

    pairs = n_dp // 2
    rows = slots * tile
    numbers = jnp.stack([tile_ids[0] // cols, tile_ids[0] % cols]).astype(jnp.bfloat16)
    numbers = jnp.pad(numbers, ((0, TAIL - 2), (0, tile - slots)))
    packed = jnp.concatenate([masked.reshape(rows, tile), numbers], axis=0)
    dma = pltpu.SemaphoreType.DMA
    in_hbm = pl.BlockSpec(memory_space=pl.ANY)
    in_vmem = pl.BlockSpec(memory_space=pltpu.VMEM)
    weights, grads, normed, flipped, inverse, tails = pl.pallas_call(
        functools.partial(spread_kernel, pairs=pairs, n_tensor=n_tensor, tile=tile),
        out_shape=(
            jax.ShapeDtypeStruct((n_dp, n_tensor, rows + TAIL, tile), jnp.bfloat16),
            jax.ShapeDtypeStruct((n_tensor, tokens, part_cols), jnp.bfloat16),
            jax.ShapeDtypeStruct((tokens, width), jnp.bfloat16),
            jax.ShapeDtypeStruct((width, tokens), jnp.bfloat16),
            jax.ShapeDtypeStruct((tokens, 1), jnp.float32),
            jax.ShapeDtypeStruct((n_dp, n_tensor, TAIL, tile), jnp.bfloat16),
        ),
        in_specs=[in_hbm, in_hbm, in_vmem, in_vmem],
        out_specs=[in_hbm, in_hbm, in_vmem, in_vmem, in_vmem, in_vmem],
        scratch_shapes=[
            dma((n_tensor,)), dma((n_tensor,)), dma((n_tensor,)),
            dma((n_tensor, pairs)), dma((n_tensor, pairs)),
            dma((n_tensor, pairs)), dma((n_tensor, pairs)),
            dma((n_tensor,)), dma((n_tensor,)), dma((3,)),
        ],
        compiler_params=pltpu.CompilerParams(
            collective_id=0, has_side_effects=True, vmem_limit_bytes=VMEM_BYTES
        ),
        name="spread",
    )(packed, proj_grad.reshape(n_tensor, tokens, part_cols), hidden, norm_gain[None, :])
    numbers = tails[:, :, :2, :slots].astype(jnp.int32)
    ids = numbers[:, :, 0] * cols + numbers[:, :, 1]

    whole = lambda *shape: pl.BlockSpec(shape, lambda t, ids: (0,) * len(shape))
    w_spec = pl.BlockSpec((n_dp, 1, rows + TAIL, tile), lambda t, ids: (0, t, 0, 0))
    t_spec = pl.BlockSpec((n_dp, 1, rows, tile), lambda t, ids: (0, t, 0, 0))
    c_spec = pl.BlockSpec((1, tokens, part_cols), lambda t, ids: (t, 0, 0))
    total = n_dp * n_tensor * slots
    flops = 2 * total * tokens * tile * tile
    params = pltpu.CompilerParams(
        dimension_semantics=("arbitrary",), vmem_limit_bytes=VMEM_BYTES
    )
    projected = pl.pallas_call(
        functools.partial(project_kernel, cols=cols),
        out_shape=jax.ShapeDtypeStruct((n_tensor, tokens, part_cols), jnp.bfloat16),
        grid_spec=pltpu.PrefetchScalarGridSpec(
            num_scalar_prefetch=1,
            grid=(n_tensor,),
            in_specs=[whole(tokens, width), w_spec],
            out_specs=c_spec,
            scratch_shapes=[pltpu.VMEM((tokens, part_cols), jnp.float32)],
        ),
        compiler_params=params,
        cost_estimate=pl.CostEstimate(
            flops=4 * flops, bytes_accessed=2 * total * tile * tile, transcendentals=0
        ),
        name="project",
    )(ids, normed, weights)
    projected, grads = lax.optimization_barrier((projected, grads))
    projections = lax.all_to_all(projected, "tensor", split_axis=0, concat_axis=0)
    tile_parts, hidden_grad, gain_part = pl.pallas_call(
        functools.partial(gradient_kernel, cols=cols),
        out_shape=(
            jax.ShapeDtypeStruct((n_dp, n_tensor, rows, tile), jnp.bfloat16),
            jax.ShapeDtypeStruct((tokens, width), jnp.bfloat16),
            jax.ShapeDtypeStruct((1, width), jnp.float32),
        ),
        grid_spec=pltpu.PrefetchScalarGridSpec(
            num_scalar_prefetch=1,
            grid=(n_tensor,),
            in_specs=[
                whole(width, tokens), w_spec, c_spec, whole(tokens, width),
                whole(tokens, 1), whole(1, width),
            ],
            out_specs=[t_spec, whole(tokens, width), whole(1, width)],
            scratch_shapes=[pltpu.VMEM((tokens, width), jnp.float32)],
        ),
        compiler_params=params,
        cost_estimate=pl.CostEstimate(
            flops=8 * flops, bytes_accessed=4 * total * tile * tile, transcendentals=0
        ),
        name="gradient",
    )(ids, flipped, weights, grads, hidden, inverse, norm_gain[None, :])

    chunk = (n_tensor, rows, tile)
    held = 2 * (3 * pairs + 1) * n_tensor * rows * tile
    if held < VMEM_BYTES // 2:
        small = (8, width // 8)
        f32 = jnp.float32
        tile_sum, gain_grad = pl.pallas_call(
            functools.partial(collect_kernel, pairs=pairs, n_tensor=n_tensor, tile=tile),
            out_shape=(
                jax.ShapeDtypeStruct((rows, tile), f32),
                jax.ShapeDtypeStruct(small, f32),
            ),
            in_specs=[in_hbm, in_vmem],
            out_specs=[in_vmem, in_vmem],
            scratch_shapes=[
                pltpu.VMEM((pairs,) + chunk, jnp.bfloat16),
                pltpu.VMEM((pairs,) + chunk, jnp.bfloat16),
                pltpu.VMEM((pairs,) + chunk, jnp.bfloat16),
                pltpu.VMEM(chunk, jnp.bfloat16),
                pltpu.VMEM(small, f32),
                pltpu.VMEM((pairs,) + small, f32),
                pltpu.VMEM((n_tensor,) + small, f32),
                dma((pairs, n_tensor)), dma((pairs, n_tensor)),
                dma((pairs, n_tensor)), dma((pairs, n_tensor)),
                dma((n_tensor,)), dma((n_tensor,)),
                dma, dma, dma((pairs,)), dma((pairs,)), dma((n_tensor,)), dma((n_tensor,)),
                dma((pairs, n_tensor)),
            ],
            compiler_params=pltpu.CompilerParams(
                collective_id=1, has_side_effects=True, vmem_limit_bytes=VMEM_BYTES
            ),
            name="collect",
        )(tile_parts, gain_part.reshape(small))
        gain_grad = gain_grad.reshape(width)
    else:
        plane = lax.psum_scatter(tile_parts, "dp", scatter_dimension=0, tiled=False)
        tile_sum = lax.psum_scatter(plane, "tensor", scatter_dimension=0, tiled=False)
        gain_grad = lax.psum(gain_part[0], ("dp", "tensor"))
    projections = projections.reshape(seq, part_cols)
    tile_sum = tile_sum.reshape(slots, tile, tile).astype(jnp.float32)
    tile_grads = jnp.where(live[:, None, None], tile_sum, 0.0)[None]
    return (projections, hidden_grad, tile_grads, gain_grad)


def solution(mesh):
    in_specs = (
        P(("dp", "tensor"), None),
        P(),
        P("tensor", "dp", None, None),
        P("tensor", "dp"),
        P("tensor", "dp"),
        P("dp", "tensor"),
    )
    out_specs = (P("dp", "tensor"), P(("dp", "tensor"), None), P("tensor", "dp", None, None), P())
    return jax.shard_map(body, mesh=mesh, in_specs=in_specs, out_specs=out_specs, check_vma=False)
```

```python
import functools

import jax
import jax.numpy as jnp
from jax import lax
from jax.experimental import pallas as pl
from jax.experimental.pallas import tpu as pltpu
from jax.sharding import PartitionSpec as P

EPSILON = 1e-05
VMEM_BYTES = 56 * 1024 * 1024
MESH = pl.DeviceIdType.MESH
TAIL = 16


def lanes(block, tile):
    return pl.ds(pl.multiple_of(block * tile, tile), tile)


def spread_kernel(
    tiles_ref, g_ref, h_ref, gain_ref,
    w_ref, grads_ref, x_ref, xt_ref, inv_ref, tail_ref,
    up_send, down_send, z_recv, p_send, p_recv, c_send, c_recv, a_send, a_recv, l_sem,
    *, pairs, n_tensor, tile,
):
    d = lax.axis_index("dp")
    t = lax.axis_index("tensor")
    core = lax.rem(d, 2)
    pair = d // 2
    other = pair * 2 + 1 - core

    def line(k):
        return lax.rem(t + k + n_tensor, n_tensor)

    def peer(j):
        return lax.rem(pair + j + pairs, pairs) * 2 + core

    greet(d, t, other, peer, line, pairs, n_tensor)

    def remote(src, dst, send, recv, to):
        return pltpu.make_async_remote_copy(
            src_ref=src, dst_ref=dst, send_sem=send, recv_sem=recv,
            device_id=to, device_id_type=MESH,
        )

    def hop(q, step, src):
        send = up_send if step > 0 else down_send
        return remote(src, w_ref.at[d, q], send.at[q], z_recv.at[q], (d, t + step))

    def over_plane(q, j, src):
        return remote(src, w_ref.at[d, q], p_send.at[q, j], p_recv.at[q, j], (peer(j), t))

    def over_core(q, j, src):
        slot = w_ref.at[peer(-j), q]
        return remote(src, slot, c_send.at[q, j], c_recv.at[q, j], (other, t))

    def exchange(k):
        return remote(
            g_ref.at[line(k)], grads_ref.at[t], a_send.at[k], a_recv.at[k], (d, line(k))
        )

    def landed(slot, send, recv):
        remote(slot, slot, send, recv, (other, t)).wait_recv()

    def share(q, src):
        for j in range(1, pairs):
            over_plane(q, j, src).start()
        over_core(q, 0, src).start()

    @pl.when(t + 1 < n_tensor)
    def _():
        hop(t, 1, tiles_ref).start()

    @pl.when(t > 0)
    def _():
        hop(t, -1, tiles_ref).start()

    share(t, tiles_ref)
    own = (
        pltpu.make_async_copy(tiles_ref, w_ref.at[d, t], l_sem.at[0]),
        pltpu.make_async_copy(g_ref.at[t], grads_ref.at[t], l_sem.at[1]),
    )
    for copy in own:
        copy.start()

    tokens, width = h_ref.shape
    rows = 16

    def norm_step(i, carry):
        at = pl.ds(pl.multiple_of(i * rows, rows), rows)
        hidden = h_ref[at, :].astype(jnp.float32)
        inverse = lax.rsqrt(jnp.mean(hidden * hidden, axis=-1, keepdims=True) + EPSILON)
        inv_ref[at, :] = inverse
        x_ref[at, :] = (hidden * inverse * gain_ref[...]).astype(x_ref.dtype)
        return carry

    lax.fori_loop(0, tokens // rows, norm_step, 0)

    for far in range(1, n_tensor):
        for step in (1, -1):
            q = t - step * far
            ends = (q >= 0) if step > 0 else (q < n_tensor)
            more = (t + 1 < n_tensor) if step > 0 else (t > 0)

            @pl.when(ends)
            def _(q=q, step=step, more=more):
                slot = w_ref.at[d, q]
                landed(slot, p_send.at[q, 0], z_recv.at[q])

                @pl.when(more)
                def _():
                    hop(q, step, slot).start()

                share(q, slot)

        if far == 1:
            for k in range(1, n_tensor):
                exchange(k).start()

    def flip_step(i, carry):
        at = lanes(i, tile)
        xt_ref[at, :] = x_ref[:, at].astype(jnp.float32).T.astype(xt_ref.dtype)
        return carry

    lax.fori_loop(0, width // tile, flip_step, 0)

    def relay(q):
        for j in range(1, pairs):
            slot = w_ref.at[peer(-j), q]
            landed(slot, p_send.at[q, j], p_recv.at[q, j])
            over_core(q, j, slot).start()

    relay(t)
    for far in range(1, n_tensor):
        for step in (1, -1):
            q = t - step * far

            @pl.when((q >= 0) if step > 0 else (q < n_tensor))
            def _(q=q):
                relay(q)

    for k in range(n_tensor):
        q = line(-k)
        for j in range(pairs):
            far = lax.rem(pair - j + pairs, pairs) * 2 + 1 - core
            landed(w_ref.at[far, q], c_send.at[q, j], c_recv.at[q, j])
    for copy in own:
        copy.wait()
    tails = pltpu.make_async_copy(
        w_ref.at[:, :, pl.ds(w_ref.shape[2] - TAIL, TAIL), :], tail_ref, l_sem.at[2]
    )
    tails.start()
    for k in range(1, n_tensor):
        landed(grads_ref.at[line(-k)], a_send.at[k], a_recv.at[k])
    tails.wait()
    for q in range(n_tensor):

        @pl.when((q <= t) & (t + 1 < n_tensor))
        def _(q=q):
            hop(q, 1, w_ref.at[d, q]).wait_send()

        @pl.when((q >= t) & (t > 0))
        def _(q=q):
            hop(q, -1, w_ref.at[d, q]).wait_send()

        if q:
            exchange(q).wait_send()
        for j in range(pairs):
            if j:
                over_plane(q, j, w_ref.at[d, q]).wait_send()
            over_core(q, j, w_ref.at[peer(-j), q]).wait_send()


def greet(d, t, other, peer, line, pairs, n_tensor):
    barrier = pltpu.get_barrier_semaphore()
    targets = [(other, t)]
    targets += [(peer(j), t) for j in range(1, pairs)]
    targets += [(d, line(k)) for k in range(1, n_tensor)]
    for target in targets:
        pl.semaphore_signal(barrier, inc=1, device_id=target, device_id_type=MESH)
    pl.semaphore_wait(barrier, len(targets))


def collect_kernel(
    parts_ref, gain_ref, sum_ref, total_ref,
    mine, from_core, from_plane, from_line, g_core, g_plane, g_line,
    c_send, c_recv, p_send, p_recv, z_send, z_recv,
    gc_send, gc_recv, gp_send, gp_recv, gz_send, gz_recv, l_sem,
    *, pairs, n_tensor, tile,
):
    d = lax.axis_index("dp")
    t = lax.axis_index("tensor")
    core = lax.rem(d, 2)
    pair = d // 2
    other = pair * 2 + 1 - core

    def line(k):
        return lax.rem(t + k + n_tensor, n_tensor)

    def near(j):
        return lax.rem(pair + j + pairs, pairs)

    def peer(j):
        return near(j) * 2 + core

    greet(d, t, other, peer, line, pairs, n_tensor)

    def remote(src, dst, send, recv, to):
        return pltpu.make_async_remote_copy(
            src_ref=src, dst_ref=dst, send_sem=send, recv_sem=recv,
            device_id=to, device_id_type=MESH,
        )

    def over_core(j, k):
        return remote(
            parts_ref.at[near(j) * 2 + 1 - core, line(k)], from_core.at[near(j), line(k)],
            c_send.at[j, k], c_recv.at[j, k], (other, t),
        )

    def load_own(j, k):
        return pltpu.make_async_copy(
            parts_ref.at[peer(j), line(k)], mine.at[near(j), line(k)], l_sem.at[j, k]
        )

    def own_landed(j, k):
        load_own(j, k).wait()
        landed(from_core.at[near(j), line(k)], c_send.at[j, k], c_recv.at[j, k])

    def over_plane(j, k):
        return remote(
            mine.at[near(j), line(k)], from_plane.at[pair, line(k)],
            p_send.at[j, k], p_recv.at[j, k], (peer(j), t),
        )

    def over_line(k):
        return remote(
            mine.at[pair, line(k)], from_line.at[k], z_send.at[k], z_recv.at[k], (d, line(k))
        )

    def landed(slot, send, recv):
        remote(slot, slot, send, recv, (other, t)).wait_recv()

    order = list(range(1, pairs)) + [0]
    gain_core = remote(gain_ref, g_core, gc_send, gc_recv, (other, t))
    gain_core.start()
    lines = list(range(1, n_tensor)) + [0]
    for k in lines:
        for j in order:
            over_core(j, k).start()
            load_own(j, k).start()

    gain_core.wait_recv()
    g_plane[pair] = gain_ref[...] + g_core[...]
    gain_plane = [
        remote(g_plane.at[pair], g_plane.at[pair], gp_send.at[j], gp_recv.at[j], (peer(j), t))
        for j in range(1, pairs)
    ]
    for copy in gain_plane:
        copy.start()

    steps = mine.shape[2] // tile
    f32 = jnp.float32
    for k in lines:
        for j in range(1, pairs):
            own_landed(j, k)

            def core_step(i, carry, j=j, k=k):
                at = lanes(i, tile)
                both = mine[near(j), line(k), at, :].astype(f32)
                both += from_core[near(j), line(k), at, :].astype(f32)
                mine[near(j), line(k), at, :] = both.astype(mine.dtype)
                return carry

            lax.fori_loop(0, steps, core_step, 0)
            over_plane(j, k).start()

    for j in range(1, pairs):
        landed(g_plane.at[near(-j)], gp_send.at[j], gp_recv.at[j])
    whole_plane = g_plane[0]
    for p in range(1, pairs):
        whole_plane += g_plane[p]
    g_line[t] = whole_plane
    gain_line = [
        remote(g_line.at[t], g_line.at[t], gz_send.at[k], gz_recv.at[k], (d, line(k)))
        for k in range(1, n_tensor)
    ]
    for copy in gain_line:
        copy.start()

    for k in lines:
        own_landed(0, k)
        for j in range(1, pairs):
            landed(from_plane.at[near(-j), line(k)], p_send.at[j, k], p_recv.at[j, k])

        def plane_step(i, carry, k=k):
            at = lanes(i, tile)
            total = mine[pair, line(k), at, :].astype(f32)
            total += from_core[pair, line(k), at, :].astype(f32)
            for j in range(1, pairs):
                total += from_plane[near(-j), line(k), at, :].astype(f32)
            if k:
                mine[pair, line(k), at, :] = total.astype(mine.dtype)
            else:
                sum_ref[at, :] = total
            return carry

        lax.fori_loop(0, steps, plane_step, 0)
        if k:
            over_line(k).start()

    for k in range(1, n_tensor):
        landed(g_line.at[line(-k)], gz_send.at[k], gz_recv.at[k])
    whole_line = g_line[0]
    for q in range(1, n_tensor):
        whole_line += g_line[q]
    total_ref[...] = whole_line

    for k in range(1, n_tensor):
        landed(from_line.at[k], z_send.at[k], z_recv.at[k])

    def line_step(i, carry):
        at = lanes(i, tile)
        total = sum_ref[at, :]
        for k in range(1, n_tensor):
            total += from_line[k, at, :].astype(f32)
        sum_ref[at, :] = total
        return carry

    lax.fori_loop(0, steps, line_step, 0)

    gain_core.wait_send()
    for copy in gain_plane + gain_line:
        copy.wait_send()
    for j in range(pairs):
        for k in range(n_tensor):
            over_core(j, k).wait_send()
            if j:
                over_plane(j, k).wait_send()
    for k in range(1, n_tensor):
        over_line(k).wait_send()


def project_kernel(ids_ref, x_ref, w_ref, out_ref, acc_ref, *, cols):
    owners, slots = ids_ref.shape[0], ids_ref.shape[2]
    tile = w_ref.shape[-1]
    t = pl.program_id(0)
    acc_ref[...] = jnp.zeros_like(acc_ref)

    def owner_step(owner, carry):
        parts = []
        for s in range(slots):
            block = ids_ref[owner, t, s]
            left = x_ref[:, lanes(block // cols, tile)]
            parts.append(jnp.dot(left, w_ref[owner, 0, s * tile:(s + 1) * tile, :], preferred_element_type=jnp.float32))
        for s in range(slots):
            place = lanes(ids_ref[owner, t, s] % cols, tile)
            acc_ref[:, place] += parts[s]
        return carry

    lax.fori_loop(0, owners, owner_step, 0)
    out_ref[0] = acc_ref[...].astype(out_ref.dtype)


def gradient_kernel(
    ids_ref, xt_ref, w_ref, g_ref, h_ref, inv_ref, gain_ref,
    tiles_ref, hgrad_ref, gpart_ref, acc_ref, *, cols,
):
    owners, slots = ids_ref.shape[0], ids_ref.shape[2]
    tile = w_ref.shape[-1]
    tokens, width = acc_ref.shape
    t = pl.program_id(0)

    @pl.when(t == 0)
    def _():
        acc_ref[...] = jnp.zeros_like(acc_ref)

    def owner_step(owner, carry):
        parts = []
        for s in range(slots):
            block = ids_ref[owner, t, s]
            g = g_ref[0, :, lanes(block % cols, tile)]
            parts.append(
                lax.dot_general(
                    g, w_ref[owner, 0, s * tile:(s + 1) * tile, :], (((1,), (1,)), ((), ())),
                    preferred_element_type=jnp.float32,
                )
            )
            left = xt_ref[lanes(block // cols, tile), :]
            tiles_ref[owner, 0, s * tile:(s + 1) * tile, :] = jnp.dot(left, g, preferred_element_type=jnp.float32).astype(
                tiles_ref.dtype
            )
        for s in range(slots):
            place = lanes(ids_ref[owner, t, s] // cols, tile)
            acc_ref[:, place] += parts[s]
        return carry

    lax.fori_loop(0, owners, owner_step, 0)

    @pl.when(t == pl.num_programs(0) - 1)
    def _():
        rows = 16
        gpart_ref[...] = jnp.zeros_like(gpart_ref)

        def row_step(i, carry):
            at = pl.ds(pl.multiple_of(i * rows, rows), rows)
            inverse = inv_ref[at, :]
            unit = h_ref[at, :].astype(jnp.float32) * inverse
            row_grad = acc_ref[at, :]
            product = row_grad * unit
            gpart_ref[...] += jnp.sum(product, axis=0, keepdims=True)
            mean = jnp.mean(product * gain_ref[...], axis=-1, keepdims=True)
            hgrad_ref[at, :] = (
                inverse * (row_grad * gain_ref[...] - unit * mean)
            ).astype(hgrad_ref.dtype)
            return carry

        lax.fori_loop(0, tokens // rows, row_step, 0)


def body(hidden, norm_gain, tile_values, tile_ids, tile_counts, proj_grad):
    tokens, width = hidden.shape
    _, slots, tile, _ = tile_values.shape
    seq, part_cols = proj_grad.shape
    cols = part_cols // tile
    n_tensor = lax.axis_size("tensor")
    n_dp = lax.axis_size("dp")
    live = jnp.arange(slots) < tile_counts[0, 0]
    masked = jnp.where(live[:, None, None], tile_values[0], 0)

    pairs = n_dp // 2
    rows = slots * tile
    numbers = jnp.stack([tile_ids[0] // cols, tile_ids[0] % cols]).astype(jnp.bfloat16)
    numbers = jnp.pad(numbers, ((0, TAIL - 2), (0, tile - slots)))
    packed = jnp.concatenate([masked.reshape(rows, tile), numbers], axis=0)
    dma = pltpu.SemaphoreType.DMA
    in_hbm = pl.BlockSpec(memory_space=pl.ANY)
    in_vmem = pl.BlockSpec(memory_space=pltpu.VMEM)
    weights, grads, normed, flipped, inverse, tails = pl.pallas_call(
        functools.partial(spread_kernel, pairs=pairs, n_tensor=n_tensor, tile=tile),
        out_shape=(
            jax.ShapeDtypeStruct((n_dp, n_tensor, rows + TAIL, tile), jnp.bfloat16),
            jax.ShapeDtypeStruct((n_tensor, tokens, part_cols), jnp.bfloat16),
            jax.ShapeDtypeStruct((tokens, width), jnp.bfloat16),
            jax.ShapeDtypeStruct((width, tokens), jnp.bfloat16),
            jax.ShapeDtypeStruct((tokens, 1), jnp.float32),
            jax.ShapeDtypeStruct((n_dp, n_tensor, TAIL, tile), jnp.bfloat16),
        ),
        in_specs=[in_hbm, in_hbm, in_vmem, in_vmem],
        out_specs=[in_hbm, in_hbm, in_vmem, in_vmem, in_vmem, in_vmem],
        scratch_shapes=[
            dma((n_tensor,)), dma((n_tensor,)), dma((n_tensor,)),
            dma((n_tensor, pairs)), dma((n_tensor, pairs)),
            dma((n_tensor, pairs)), dma((n_tensor, pairs)),
            dma((n_tensor,)), dma((n_tensor,)), dma((3,)),
        ],
        compiler_params=pltpu.CompilerParams(
            collective_id=0, has_side_effects=True, vmem_limit_bytes=VMEM_BYTES
        ),
        name="spread",
    )(packed, proj_grad.reshape(n_tensor, tokens, part_cols), hidden, norm_gain[None, :])
    numbers = tails[:, :, :2, :slots].astype(jnp.int32)
    ids = numbers[:, :, 0] * cols + numbers[:, :, 1]

    whole = lambda *shape: pl.BlockSpec(shape, lambda t, ids: (0,) * len(shape))
    w_spec = pl.BlockSpec((n_dp, 1, rows + TAIL, tile), lambda t, ids: (0, t, 0, 0))
    t_spec = pl.BlockSpec((n_dp, 1, rows, tile), lambda t, ids: (0, t, 0, 0))
    c_spec = pl.BlockSpec((1, tokens, part_cols), lambda t, ids: (t, 0, 0))
    total = n_dp * n_tensor * slots
    flops = 2 * total * tokens * tile * tile
    params = pltpu.CompilerParams(
        dimension_semantics=("arbitrary",), vmem_limit_bytes=VMEM_BYTES
    )
    projected = pl.pallas_call(
        functools.partial(project_kernel, cols=cols),
        out_shape=jax.ShapeDtypeStruct((n_tensor, tokens, part_cols), jnp.bfloat16),
        grid_spec=pltpu.PrefetchScalarGridSpec(
            num_scalar_prefetch=1,
            grid=(n_tensor,),
            in_specs=[whole(tokens, width), w_spec],
            out_specs=c_spec,
            scratch_shapes=[pltpu.VMEM((tokens, part_cols), jnp.float32)],
        ),
        compiler_params=params,
        cost_estimate=pl.CostEstimate(
            flops=4 * flops, bytes_accessed=2 * total * tile * tile, transcendentals=0
        ),
        name="project",
    )(ids, normed, weights)
    projected, grads = lax.optimization_barrier((projected, grads))
    projections = lax.all_to_all(projected, "tensor", split_axis=0, concat_axis=0)
    tile_parts, hidden_grad, gain_part = pl.pallas_call(
        functools.partial(gradient_kernel, cols=cols),
        out_shape=(
            jax.ShapeDtypeStruct((n_dp, n_tensor, rows, tile), jnp.bfloat16),
            jax.ShapeDtypeStruct((tokens, width), jnp.bfloat16),
            jax.ShapeDtypeStruct((1, width), jnp.float32),
        ),
        grid_spec=pltpu.PrefetchScalarGridSpec(
            num_scalar_prefetch=1,
            grid=(n_tensor,),
            in_specs=[
                whole(width, tokens), w_spec, c_spec, whole(tokens, width),
                whole(tokens, 1), whole(1, width),
            ],
            out_specs=[t_spec, whole(tokens, width), whole(1, width)],
            scratch_shapes=[pltpu.VMEM((tokens, width), jnp.float32)],
        ),
        compiler_params=params,
        cost_estimate=pl.CostEstimate(
            flops=8 * flops, bytes_accessed=4 * total * tile * tile, transcendentals=0
        ),
        name="gradient",
    )(ids, flipped, weights, grads, hidden, inverse, norm_gain[None, :])

    chunk = (n_tensor, rows, tile)
    held = 2 * (3 * pairs + 1) * n_tensor * rows * tile
    if held < VMEM_BYTES // 2:
        small = (8, width // 8)
        f32 = jnp.float32
        tile_sum, gain_grad = pl.pallas_call(
            functools.partial(collect_kernel, pairs=pairs, n_tensor=n_tensor, tile=tile),
            out_shape=(
                jax.ShapeDtypeStruct((rows, tile), f32),
                jax.ShapeDtypeStruct(small, f32),
            ),
            in_specs=[in_hbm, in_vmem],
            out_specs=[in_vmem, in_vmem],
            scratch_shapes=[
                pltpu.VMEM((pairs,) + chunk, jnp.bfloat16),
                pltpu.VMEM((pairs,) + chunk, jnp.bfloat16),
                pltpu.VMEM((pairs,) + chunk, jnp.bfloat16),
                pltpu.VMEM(chunk, jnp.bfloat16),
                pltpu.VMEM(small, f32),
                pltpu.VMEM((pairs,) + small, f32),
                pltpu.VMEM((n_tensor,) + small, f32),
                dma((pairs, n_tensor)), dma((pairs, n_tensor)),
                dma((pairs, n_tensor)), dma((pairs, n_tensor)),
                dma((n_tensor,)), dma((n_tensor,)),
                dma, dma, dma((pairs,)), dma((pairs,)), dma((n_tensor,)), dma((n_tensor,)),
                dma((pairs, n_tensor)),
            ],
            compiler_params=pltpu.CompilerParams(
                collective_id=1, has_side_effects=True, vmem_limit_bytes=VMEM_BYTES
            ),
            name="collect",
        )(tile_parts, gain_part.reshape(small))
        gain_grad = gain_grad.reshape(width)
    else:
        plane = lax.psum_scatter(tile_parts, "dp", scatter_dimension=0, tiled=False)
        tile_sum = lax.psum_scatter(plane, "tensor", scatter_dimension=0, tiled=False)
        gain_grad = lax.psum(gain_part[0], ("dp", "tensor"))
    projections = projections.reshape(seq, part_cols)
    tile_sum = tile_sum.reshape(slots, tile, tile).astype(jnp.float32)
    tile_grads = jnp.where(live[:, None, None], tile_sum, 0.0)[None]
    return (projections, hidden_grad, tile_grads, gain_grad)


def solution(mesh):
    in_specs = (
        P(("dp", "tensor"), None),
        P(),
        P("tensor", "dp", None, None),
        P("tensor", "dp"),
        P("tensor", "dp"),
        P("dp", "tensor"),
    )
    out_specs = (P("dp", "tensor"), P(("dp", "tensor"), None), P("tensor", "dp", None, None), P())
    return jax.shard_map(body, mesh=mesh, in_specs=in_specs, out_specs=out_specs, check_vma=False)
```
